32 devices in a mesh: gx: 4 (over x, core), gy: 8 (over z, y).
Axes of the slice: x: 2, y: 2, z: 4, core: 2. Of those that a mesh axis runs over, the one named last changes fastest.
Arguments:
- intensity: float32 [32, 512, 1024], P(None, 'gx', 'gy'), may hold values from -6 to 6
- weight: float32 [32, 512, 1024], P(None, 'gx', 'gy'), may hold values from 0.2 to 5
- spacing: int32 [3], replicated, may hold values from 10 to 12
- anchor: int32 [3], replicated, may hold values from 0 to 5
- reach: int32 [1], replicated, may hold values from 36 to 49
Outputs:
- delta_pdf: float32 [32, 512, 1024], P('gx', 'gy')
The draws below stay inside these ranges and needn't reach their ends.
All inputs are finite; a program needn't handle non-finite values.
Results may differ from the reference program's by a relative error of at most 0.00007.
Values sent between devices are 32-bit elements; how exact they have to be, the bound alone decides.
No kernel may reach another device: no remote copies, remote signals or barrier semaphores. Data moves between devices by JAX's collectives and lax.ppermute only.
A program may use at most 128 MiB of HBM per device.

```python
import math
import jax
import jax.numpy as jnp
from jax import lax

NZ = 32
NX = 512
NY = 1024


def block_scale(own_key, dims, pieces, smallest, largest):
    def one(axis_at, shards_of):
        draws = jax.random.uniform(jax.random.fold_in(jax.random.fold_in(own_key, 6), axis_at), (shards_of,), jnp.float32, smallest / len(pieces), largest / len(pieces))
        return jnp.repeat(jnp.exp(draws), dims[axis_at] // shards_of).reshape((-1,) + (1,) * (len(dims) - axis_at - 1))

    gain = one(*pieces[0])
    for cut in pieces[1:]:
        gain = gain * one(*cut)
    return gain


def centred(key, dims, deviation, limit, split=(), kind=jnp.bfloat16):
    result = deviation * jax.random.normal(key, dims, jnp.float32)
    if split:
        result = result * block_scale(key, dims, split, -0.22, 0.18)
    return jnp.clip(result, -limit, limit).astype(kind)


def setup_inputs(seed: int = 0) -> dict:
    key_of = jax.random.split(jax.random.key(seed), 6)
    intensity = centred(key_of[0], (NZ, NX, NY), 1.0, 6.0, ((1, 4), (2, 8)), jnp.float32)
    weight = jnp.clip(jnp.exp(math.log(5.0) - 3.218876 * jax.random.uniform(key_of[1], (NZ, NX, NY), jnp.float32) ** block_scale(key_of[1], (NZ, NX, NY), ((1, 4), (2, 8)), -0.2, 0.2)), 0.2, 5.0)
    spacing = jax.random.randint(key_of[2], (3,), 10, 13).astype(jnp.int32)
    anchor = jax.random.randint(key_of[3], (3,), 0, 6).astype(jnp.int32)
    reach = jax.random.randint(key_of[4], (1,), 36, 50).astype(jnp.int32)
    return {"intensity": intensity, "weight": weight, "spacing": spacing, "anchor": anchor, "reach": reach}


taps_coef = ((1.0, 2.0, 1.0), (2.0, 4.0, 2.0), (1.0, 2.0, 1.0))

def plane_dist(position, spacing, anchor):
    offset = jnp.mod(position - anchor, spacing)
    return jnp.minimum(offset, spacing - offset)

def punch_holes(zpos, xpos, ypos, spacing, anchor, reach, limit_x, limit_y):
    dist_z = plane_dist(zpos, spacing[0], anchor[0])
    dist_x = plane_dist(xpos, spacing[1], anchor[1])
    dist_y = plane_dist(ypos, spacing[2], anchor[2])
    plane = (dist_x * dist_x)[:, None] + (dist_y * dist_y)[None, :]
    inside_x = (xpos >= 0) & (xpos < limit_x)
    inside_y = (ypos >= 0) & (ypos < limit_y)
    flat = (plane <= reach[0]) & inside_x[:, None] & inside_y[None, :]
    return (dist_z <= 1)[:, None, None] & flat[None, :, :]

def sweep(values_ext, weight_ext, holes):
    size_x = values_ext.shape[1] - 2
    size_y = values_ext.shape[2] - 2
    weighted = None
    total_weight = None
    for row_off in range(3):
        for col_off in range(3):
            near_weight = taps_coef[row_off][col_off] * weight_ext[:, row_off:row_off + size_x, col_off:col_off + size_y]
            term = near_weight * values_ext[:, row_off:row_off + size_x, col_off:col_off + size_y]
            weighted = term if weighted is None else weighted + term
            total_weight = near_weight if total_weight is None else total_weight + near_weight
    centre = values_ext[:, 1:1 + size_x, 1:1 + size_y]
    return jnp.where(holes, weighted / jnp.where(holes, total_weight, 1.0), centre)

def cosine_rows(start, count, length):
    freq = start + jnp.arange(count, dtype=jnp.int32)
    place = 2 * jnp.arange(length, dtype=jnp.int32) + 1
    phase = jnp.mod(freq[:, None] * place[None, :], 4 * length).astype(jnp.float32)
    return jnp.cos(phase * (math.pi / (2 * length))) * math.sqrt(2.0 / length)

def reference(intensity, weight, spacing, anchor, reach):
    holes = punch_holes(jnp.arange(NZ, dtype=jnp.int32), jnp.arange(NX, dtype=jnp.int32), jnp.arange(NY, dtype=jnp.int32), spacing, anchor, reach, NX, NY)
    values = jnp.where(holes, 0.0, intensity)
    pad_width = ((0, 0), (1, 1), (1, 1))
    weight_ext = jnp.pad(weight, pad_width)
    for level in range(3):
        values = sweep(jnp.pad(values, pad_width), weight_ext, holes)
    spectrum_x = jnp.einsum('kx,zxy->zky', cosine_rows(0, NX, NX), values, precision=lax.Precision.HIGHEST)
    return jnp.einsum('zxy,ky->zxk', spectrum_x, cosine_rows(0, NY, NY), precision=lax.Precision.HIGHEST)
```

```python
import functools
import math

import jax
import jax.numpy as jnp
import numpy as np
from jax import lax
from jax.experimental import pallas as pl
from jax.experimental.pallas import tpu as pltpu
from jax.sharding import PartitionSpec as P

MIN_SPACING = 10
HALO = 3
LANES = 128
VMEM_LIMIT = 40 * 1024 * 1024
ANY = pl.BlockSpec(memory_space=pl.ANY)
SMEM = pl.BlockSpec(memory_space=pltpu.SMEM)
VMEM = pl.BlockSpec(memory_space=pltpu.VMEM)


def hole_slots(depth):
    whole, left = divmod(depth, MIN_SPACING)
    return min(depth, 3 * whole + min(3, left))


def clean_chunks(count):
    first = min(2, count)
    return [part for part in (first, count - first) if part]


@functools.lru_cache(maxsize=None)
def cosine_split(length):
    freq = np.arange(length, dtype=np.int64)
    phase = (freq[:, None] * (2 * freq[None, :] + 1)) % (4 * length)
    matrix = np.cos(phase * (math.pi / (2 * length))) * math.sqrt(2.0 / length)
    high = matrix.astype(jnp.bfloat16)
    low = (matrix - high.astype(np.float64)).astype(jnp.bfloat16)
    return high, low


def split(value):
    high = value.astype(jnp.bfloat16)
    return high, (value - high.astype(jnp.float32)).astype(jnp.bfloat16)


def params(**more):
    return pltpu.CompilerParams(vmem_limit_bytes=VMEM_LIMIT, **more)


def floor_mod(value, by):
    rest = lax.rem(value, by)
    return jnp.where(rest < 0, rest + by, rest)


def order_layers(table, at, first, depth, spacing, anchor):
    phase = floor_mod(first - anchor, spacing)
    front = jnp.int32(0)
    back = jnp.int32(depth - 1)
    for step in range(depth):
        hole = (phase <= 1) | (phase == spacing - 1)
        table[at + jnp.where(hole, back, front)] = first + step
        front = jnp.where(hole, front, front + 1)
        back = jnp.where(hole, back - 1, back)
        phase = jnp.where(phase + 1 == spacing, 0, phase + 1)


def is_hole_layer(layer, spacing, anchor):
    phase = floor_mod(layer - anchor, spacing)
    return (phase <= 1) | (phase == spacing - 1)


def squared_dist(position, spacing, anchor):
    step = spacing.astype(jnp.float32)
    from_anchor = (position - anchor).astype(jnp.float32)
    turns = jnp.floor((from_anchor + 0.5) / step)
    offset = from_anchor - turns * step
    dist = jnp.minimum(offset, step - offset)
    return dist * dist


def gather_kernel(sizes, slot, count, spacing, anchor, layers, *rest):
    groups, depth = sizes
    outs, (table, sems) = rest[:groups], rest[groups:]
    me = lax.axis_index("gx")
    for group in range(groups):
        order_layers(table, group * depth, group * depth, depth, spacing[0], anchor[0])
    copies = []
    for k in range(groups):
        for part in range(count):
            layer = table[(me ^ k) * depth + slot + part]
            copies.append(
                pltpu.make_async_copy(layers.at[layer], outs[k].at[part], sems.at[k * count + part])
            )
    for copy in copies:
        copy.start()
    for copy in copies:
        copy.wait()


def gather_clean(spacing, anchor, layers, groups, slot, count):
    depth = layers.shape[0] // groups
    return pl.pallas_call(
        functools.partial(gather_kernel, (groups, depth), slot, count),
        out_shape=[jax.ShapeDtypeStruct((count,) + layers.shape[1:], jnp.float32)] * groups,
        in_specs=[SMEM, SMEM, ANY],
        out_specs=[ANY] * groups,
        scratch_shapes=[
            pltpu.SMEM((groups * depth,), jnp.int32),
            pltpu.SemaphoreType.DMA((groups * count,)),
        ],
        compiler_params=params(),
        name="gather_clean",
    )(spacing, anchor, layers)


def punch_kernel(sizes, spacing, anchor, reach, layers, weights, v_out, w_out, first_out, last_out, table, sems):
    groups, depth, held = sizes
    rows = v_out.shape[1]
    total = groups * held
    x_start = lax.axis_index("gx") * rows
    y_start = lax.axis_index("gy") * LANES
    for group in range(groups):
        order_layers(table, group * depth, group * depth, depth, spacing[0], anchor[0])
    copies = []
    for at in range(total):
        layer = table[(at // held) * depth + depth - held + at % held]
        copies.append(pltpu.make_async_copy(layers.at[layer], v_out.at[at], sems.at[at]))
        copies.append(pltpu.make_async_copy(weights.at[layer], w_out.at[at], sems.at[total + at]))
    for copy in copies:
        copy.start()
    shape = (rows, LANES)
    x_at = x_start + lax.broadcasted_iota(jnp.int32, shape, 0)
    lane = lax.broadcasted_iota(jnp.int32, shape, 1)
    plane = squared_dist(x_at, spacing[1], anchor[1]) + squared_dist(y_start + lane, spacing[2], anchor[2])
    flat = plane <= reach[0].astype(jnp.float32)
    for copy in copies:
        copy.wait()
    per_pack = LANES // HALO
    first = last = None
    for at in range(2 * total):
        if at < total:
            layer = table[(at // held) * depth + depth - held + at % held]
            tall = jnp.where(is_hole_layer(layer, spacing[0], anchor[0]), 1.0, 0.0)
            tile = jnp.where(flat & (jnp.full(shape, tall) > 0.5), 0.0, v_out[at])
            v_out[at] = tile
        else:
            tile = w_out[at - total]
        place = at % per_pack
        if place == 0:
            first = tile
            last = pltpu.roll(tile, HALO, 1)
        else:
            here = (lane >= HALO * place) & (lane < HALO * place + HALO)
            first = jnp.where(here, pltpu.roll(tile, HALO * place, 1), first)
            last = jnp.where(here, pltpu.roll(tile, HALO * (place + 1), 1), last)
        if place == per_pack - 1 or at == 2 * total - 1:
            first_out[at // per_pack] = first
            last_out[at // per_pack] = last


def punch(spacing, anchor, reach, layers, weights, groups, held):
    depth = layers.shape[0] // groups
    total = groups * held
    packs = -(-2 * total // (LANES // HALO))
    tile = layers.shape[1:]
    return pl.pallas_call(
        functools.partial(punch_kernel, (groups, depth, held)),
        out_shape=[jax.ShapeDtypeStruct((count,) + tile, jnp.float32) for count in (total, total, packs, packs)],
        in_specs=[SMEM, SMEM, SMEM, ANY, ANY],
        out_specs=[VMEM] * 4,
        scratch_shapes=[
            pltpu.SMEM((groups * depth,), jnp.int32),
            pltpu.SemaphoreType.DMA((2 * total,)),
        ],
        compiler_params=params(),
        name="punch",
    )(spacing, anchor, reach, layers, weights)


def edge_kernel(v, w, left, right, top, bottom):
    rows = v.shape[1]
    at = 0
    for ref in (v, w, left, right):
        count = ref.shape[0]
        top[at : at + count] = ref[:, :8]
        bottom[at : at + count] = ref[:, rows - 8 :]
        at += count


def edges(v, w, left, right):
    count = 2 * (v.shape[0] + left.shape[0])
    return pl.pallas_call(
        edge_kernel,
        out_shape=[jax.ShapeDtypeStruct((count, 8, LANES), jnp.float32)] * 2,
        in_specs=[VMEM] * 4,
        out_specs=[VMEM] * 2,
        compiler_params=params(),
        name="edges",
    )(v, w, left, right)


def fill_kernel(sizes, spacing, anchor, reach, v_in, w_in, left, right, above, below, *rest):
    groups, depth, held, full_x, full_y = sizes
    outs, (table, result) = rest[:groups], rest[groups:]
    total = groups * held
    packs = left.shape[0]
    rows = v_in.shape[1]
    me = lax.axis_index("gx")
    x_start = me * rows
    y_start = lax.axis_index("gy") * LANES
    for group in range(groups):
        order_layers(table, group * depth, group * depth, depth, spacing[0], anchor[0])
    tall = rows + 16
    shape = (tall, 2 * LANES)
    lane = lax.broadcasted_iota(jnp.int32, shape, 1)
    x_at = x_start - 8 + lax.broadcasted_iota(jnp.int32, shape, 0)
    y_at = y_start + jnp.where(lane < LANES + LANES // 2, lane, lane - 2 * LANES)
    plane = squared_dist(x_at, spacing[1], anchor[1]) + squared_dist(y_at, spacing[2], anchor[2])
    inside = (x_at >= 0) & (x_at < full_x) & (y_at >= 0) & (y_at < full_y)
    known = (lane < LANES + HALO) | (lane >= 2 * LANES - HALO)
    flat = (plane <= reach[0].astype(jnp.float32)) & inside & known
    flat_f = jnp.where(flat, 1.0, 0.0)
    per_pack = LANES // HALO
    edge_lane = lax.broadcasted_iota(jnp.int32, (tall, LANES), 1)

    def column(up, middle, down):
        return jnp.concatenate([up, middle, down], axis=0)

    def extended(ref, at, array):
        own = column(above[array], ref[at], below[array])
        pack = lax.div(array, per_pack)
        place = lax.rem(array, per_pack)
        at_left = 2 * total + pack
        at_right = 2 * total + packs + pack
        from_left = column(above[at_left], left[pack], below[at_left])
        from_right = column(above[at_right], right[pack], below[at_right])
        shift = HALO * place
        after = pltpu.roll(from_right, lax.rem(LANES - shift, LANES), 1)
        before = pltpu.roll(from_left, lax.rem(2 * LANES - HALO - shift, LANES), 1)
        edge = jnp.where(edge_lane < HALO, after, jnp.where(edge_lane >= LANES - HALO, before, 0.0))
        return jnp.concatenate([own, edge], axis=1)

    def smooth(value):
        value = pltpu.roll(value, 1, 0) + (value + value) + pltpu.roll(value, tall - 1, 0)
        return pltpu.roll(value, 1, 1) + (value + value) + pltpu.roll(value, 2 * LANES - 1, 1)

    def one(at, carry):
        layer = table[lax.div(at, held) * depth + depth - held + lax.rem(at, held)]
        hole_layer = is_hole_layer(layer, spacing[0], anchor[0])

        @pl.when(hole_layer)
        def _():
            value = extended(v_in, at, at)
            weight = extended(w_in, at, total + at)
            hole = flat_f > 0.5
            inverse = 1.0 / jnp.where(hole, smooth(weight), 1.0)
            for _ in range(3):
                value = jnp.where(hole, smooth(weight * value) * inverse, value)
            result[at] = value[8 : 8 + rows, :LANES]

        @pl.when(jnp.logical_not(hole_layer))
        def _():
            result[at] = v_in[at]

        return carry

    lax.fori_loop(0, total, one, 0)
    for k in range(groups):
        outs[k][...] = result[pl.ds((me ^ k) * held, held)]


def fill(spacing, anchor, reach, v, w, left, right, above, below, groups, held, depth, full):
    rows = v.shape[1]
    return pl.pallas_call(
        functools.partial(fill_kernel, (groups, depth, held) + full),
        out_shape=[jax.ShapeDtypeStruct((held, rows, LANES), jnp.float32)] * groups,
        in_specs=[SMEM] * 3 + [VMEM] * 6,
        out_specs=[VMEM] * groups,
        scratch_shapes=[
            pltpu.SMEM((groups * depth,), jnp.int32),
            pltpu.VMEM((groups * held, rows, LANES), jnp.float32),
        ],
        compiler_params=params(),
        name="fill",
    )(spacing, anchor, reach, v, w, left, right, above, below)


def dot3(a_high, a_low, b_high, b_low, dims):
    def dot(a, b):
        return lax.dot_general(a, b, (dims, ((), ())), preferred_element_type=jnp.float32)

    return dot(a_high, b_high) + (dot(a_high, b_low) + dot(a_low, b_high))


def x_kernel(sizes, c_high, c_low, *rest):
    groups, parts, step = sizes
    pieces, outs = rest[:groups], rest[groups : groups + parts]
    b_high, b_low, acc = rest[groups + parts :]
    count, rows, _ = pieces[0].shape
    out_rows = outs[0].shape[1]
    me = lax.axis_index("gx")
    row = lax.axis_index("gy")
    tile = pl.program_id(0)

    @pl.when(tile == 0)
    def _():
        for k in range(groups):
            at = pl.ds(pl.multiple_of((me ^ k) * rows, rows), rows)
            for layer in range(count):
                high, low = split(pieces[k][layer])
                cols = pl.ds(layer * LANES, LANES)
                b_high[at, cols] = high
                b_low[at, cols] = low

    at = pl.ds(pl.multiple_of(tile * step, step), step)
    acc[at] = dot3(c_high[...], c_low[...], b_high[...], b_low[...], ((1,), (0,)))

    @pl.when(tile == pl.num_programs(0) - 1)
    def _():
        for k in range(parts):
            at = pl.ds(pl.multiple_of((row ^ k) * out_rows, out_rows), out_rows)
            for layer in range(count):
                outs[k][layer] = acc[at, pl.ds(layer * LANES, LANES)]


def along_x(pieces, parts):
    groups = len(pieces)
    count, rows, _ = pieces[0].shape
    length = rows * groups
    step = min(512, length)
    high, low = cosine_split(length)
    whole = pl.BlockSpec(pieces[0].shape, lambda n: (0, 0, 0))
    out_tile = (count, length // parts, LANES)
    return pl.pallas_call(
        functools.partial(x_kernel, (groups, parts, step)),
        grid=(length // step,),
        out_shape=[jax.ShapeDtypeStruct(out_tile, jnp.float32)] * parts,
        in_specs=[pl.BlockSpec((step, length), lambda n: (n, 0))] * 2 + [whole] * groups,
        out_specs=[pl.BlockSpec(out_tile, lambda n: (0, 0, 0))] * parts,
        scratch_shapes=[
            pltpu.VMEM((length, count * LANES), jnp.bfloat16),
            pltpu.VMEM((length, count * LANES), jnp.bfloat16),
            pltpu.VMEM((length, count * LANES), jnp.float32),
        ],
        compiler_params=params(),
        name="along_x",
    )(high, low, *pieces)


def y_kernel(sizes, slot, chained, spacing, anchor, c_high, c_low, *rest):
    parts, depth, step = sizes
    pieces = rest[:parts]
    out, a_high, a_low, acc, table, sems = rest[parts + (1 if chained else 0) :]
    count, rows, _ = pieces[0].shape
    row = lax.axis_index("gy")
    tile = pl.program_id(0)

    @pl.when(tile == 0)
    def _():
        order_layers(table, 0, lax.axis_index("gx") * depth, depth, spacing[0], anchor[0])
        for k in range(parts):
            cols = pl.ds(pl.multiple_of((row ^ k) * LANES, LANES), LANES)
            for layer in range(count):
                high, low = split(pieces[k][layer])
                at = pl.ds(layer * rows, rows)
                a_high[at, cols] = high
                a_low[at, cols] = low

    acc[tile] = dot3(a_high[...], a_low[...], c_high[...], c_low[...], ((1,), (1,)))

    def copy(n, layer):
        here = table[slot + layer] - lax.axis_index("gx") * depth
        cols = pl.ds(pl.multiple_of(n * step, step), step)
        return pltpu.make_async_copy(
            acc.at[n, pl.ds(layer * rows, rows)], out.at[here, :, cols], sems.at[n, layer]
        )

    for layer in range(count):
        copy(tile, layer).start()

    @pl.when(tile == pl.num_programs(0) - 1)
    def _():
        for n in range(acc.shape[0]):
            for layer in range(count):
                copy(n, layer).wait()


def along_y(spacing, anchor, pieces, slot, depth, before):
    parts = len(pieces)
    count, rows, _ = pieces[0].shape
    length = parts * LANES
    step = min(256, length)
    steps = length // step
    high, low = cosine_split(length)
    whole = pl.BlockSpec(pieces[0].shape, lambda n: (0, 0, 0))
    chained = before is not None
    return pl.pallas_call(
        functools.partial(y_kernel, (parts, depth, step), slot, chained),
        grid=(steps,),
        out_shape=jax.ShapeDtypeStruct((depth, rows, length), jnp.float32),
        in_specs=[SMEM, SMEM]
        + [pl.BlockSpec((step, length), lambda n: (n, 0))] * 2
        + [whole] * parts
        + ([ANY] if chained else []),
        out_specs=ANY,
        scratch_shapes=[
            pltpu.VMEM((count * rows, length), jnp.bfloat16),
            pltpu.VMEM((count * rows, length), jnp.bfloat16),
            pltpu.VMEM((steps, count * rows, step), jnp.float32),
            pltpu.SMEM((depth,), jnp.int32),
            pltpu.SemaphoreType.DMA((steps, count)),
        ],
        input_output_aliases={4 + parts: 0} if chained else {},
        compiler_params=params(),
        name="along_y",
    )(spacing, anchor, high, low, *pieces, *([before] if chained else []))


def swap(value, axis, k):
    size = lax.axis_size(axis)
    return lax.ppermute(value, axis, [(i, i ^ k) for i in range(size)])


def exchange(pieces, axis):
    got = {k: swap(pieces[k], axis, k) for k in reversed(range(1, len(pieces)))}
    return [pieces[0]] + [got[k] for k in range(1, len(pieces))]


def shift(value, axis, by):
    size = lax.axis_size(axis)
    return lax.ppermute(value, axis, [(i, i + by) for i in range(size) if 0 <= i + by < size])


def per_device(intensity, weight, spacing, anchor, reach):
    layers, rows, _ = intensity.shape
    groups = lax.axis_size("gx")
    parts = lax.axis_size("gy")
    depth = layers // groups
    held = hole_slots(depth)
    full = (rows * groups, LANES * parts)

    chunks = []
    slot = 0
    for count in clean_chunks(depth - held):
        gathered = gather_clean(spacing, anchor, intensity, groups, slot, count)
        chunks.append((slot, exchange(gathered, "gx")))
        slot += count

    v, w, first, last = punch(spacing, anchor, reach, intensity, weight, groups, held)
    left = shift(last, "gy", 1)
    right = shift(first, "gy", -1)
    top, bottom = edges(v, w, left, right)
    above = shift(bottom, "gx", 1)
    below = shift(top, "gx", -1)
    filled = fill(spacing, anchor, reach, v, w, left, right, above, below, groups, held, depth, full)
    chunks.append((slot, exchange(filled, "gx")))

    moved = [(at, exchange(along_x(pieces, parts), "gy")) for at, pieces in chunks]
    out = None
    for at, pieces in moved:
        out = along_y(spacing, anchor, pieces, at, depth, out)
    return out


def solution(mesh):
    in_specs = (P(None, "gx", "gy"), P(None, "gx", "gy"), P(), P(), P())
    out_specs = P("gx", "gy", None)
    return jax.shard_map(per_device, mesh=mesh, in_specs=in_specs, out_specs=out_specs, check_vma=False)
```

```python
import functools
import math

import jax
import jax.numpy as jnp
import numpy as np
from jax import lax
from jax.experimental import pallas as pl
from jax.experimental.pallas import tpu as pltpu
from jax.sharding import PartitionSpec as P

MIN_SPACING = 10
HALO = 3
EARLY = 5
LANES = 128
HBM = pl.BlockSpec(memory_space=pltpu.HBM)
ANY = pl.BlockSpec(memory_space=pl.ANY)
SMEM = pl.BlockSpec(memory_space=pltpu.SMEM)
VMEM = pl.BlockSpec(memory_space=pltpu.VMEM)


def hole_slots(depth):
    whole, left = divmod(depth, MIN_SPACING)
    return min(depth, 3 * whole + min(3, left))


@functools.lru_cache(maxsize=None)
def cosine_split(length):
    freq = np.arange(length, dtype=np.int64)
    phase = (freq[:, None] * (2 * freq[None, :] + 1)) % (4 * length)
    matrix = np.cos(phase * (math.pi / (2 * length))) * math.sqrt(2.0 / length)
    high = matrix.astype(jnp.bfloat16)
    low = (matrix - high.astype(np.float64)).astype(jnp.bfloat16)
    return high, low


def split(value):
    high = value.astype(jnp.bfloat16)
    return high, (value - high.astype(jnp.float32)).astype(jnp.bfloat16)


def params(length=0):
    return pltpu.CompilerParams(vmem_limit_bytes=8 * 2**20 + 6 * length * length)


def cost(micros):
    return pl.CostEstimate(flops=0, bytes_accessed=int(micros * 3.6e6), transcendentals=0)


TOKEN = jax.ShapeDtypeStruct((8, LANES), jnp.float32)


def in_hbm(value):
    return pltpu.with_memory_space_constraint(value, pltpu.HBM)


def in_vmem(value):
    return pltpu.with_memory_space_constraint(value, pltpu.VMEM)


def floor_mod(value, by):
    rest = lax.rem(value, by)
    return jnp.where(rest < 0, rest + by, rest)


def order_layers(table, at, first, depth, spacing, anchor):
    phase = floor_mod(first - anchor, spacing)
    front = jnp.int32(0)
    back = jnp.int32(depth - 1)
    for step in range(depth):
        hole = (phase <= 1) | (phase == spacing - 1)
        table[at + jnp.where(hole, back, front)] = first + step
        front = jnp.where(hole, front, front + 1)
        back = jnp.where(hole, back - 1, back)
        phase = jnp.where(phase + 1 == spacing, 0, phase + 1)


def is_hole_layer(layer, spacing, anchor):
    phase = floor_mod(layer - anchor, spacing)
    return (phase <= 1) | (phase == spacing - 1)


def squared_dist(position, spacing, anchor):
    step = spacing.astype(jnp.float32)
    from_anchor = (position - anchor).astype(jnp.float32)
    turns = jnp.floor((from_anchor + 0.5) / step)
    offset = from_anchor - turns * step
    dist = jnp.minimum(offset, step - offset)
    return dist * dist


def clean_copies(sizes, slot, count, table, layers, outs, sems):
    groups, depth = sizes
    me = lax.axis_index("gx")
    copies = []
    for k in range(groups):
        for part in range(count):
            layer = table[(me ^ k) * depth + slot + part]
            copies.append(
                pltpu.make_async_copy(layers.at[layer], outs[k].at[part], sems.at[k * count + part])
            )
    return copies


def gather_kernel(sizes, slot, count, spacing_in, anchor_in, layers, *rest):
    groups, depth = sizes
    outs, (spacing, anchor, table, sems, small) = rest[:groups], rest[groups:]
    first = pltpu.make_async_copy(spacing_in, spacing, small.at[0])
    second = pltpu.make_async_copy(anchor_in, anchor, small.at[1])
    first.start()
    second.start()
    first.wait()
    second.wait()
    for group in range(groups):
        order_layers(table, group * depth, group * depth, depth, spacing[0], anchor[0])
    copies = clean_copies(sizes, slot, count, table, layers, outs, sems)
    for copy in copies:
        copy.start()
    for copy in copies:
        copy.wait()


def gather_clean(spacing, anchor, layers, groups, slot, count):
    depth = layers.shape[0] // groups
    return pl.pallas_call(
        functools.partial(gather_kernel, (groups, depth), slot, count),
        out_shape=[jax.ShapeDtypeStruct((count,) + layers.shape[1:], jnp.float32)] * groups,
        in_specs=[HBM] * 3,
        out_specs=[VMEM] * groups,
        scratch_shapes=[
            pltpu.SMEM(spacing.shape, jnp.int32),
            pltpu.SMEM(anchor.shape, jnp.int32),
            pltpu.SMEM((groups * depth,), jnp.int32),
            pltpu.SemaphoreType.DMA((groups * count,)),
            pltpu.SemaphoreType.DMA((2,)),
        ],
        compiler_params=params(),
        cost_estimate=cost(1.5),
        name="gather_clean",
    )(in_hbm(spacing), in_hbm(anchor), in_hbm(layers))


def punch_kernel(sizes, slot, count, spacing, anchor, reach, layers, weights, v_out, w_out, first_out, last_out, *rest):
    groups, depth, held = sizes
    outs, (token, table, sems, more) = rest[: groups if count else 0], rest[-4:]
    token[...] = jnp.zeros(token.shape, jnp.float32)
    rows = v_out.shape[1]
    total = groups * held
    x_start = lax.axis_index("gx") * rows
    y_start = lax.axis_index("gy") * LANES
    for group in range(groups):
        order_layers(table, group * depth, group * depth, depth, spacing[0], anchor[0])
    copies = []
    for at in range(total):
        layer = table[(at // held) * depth + depth - held + at % held]
        copies.append(pltpu.make_async_copy(layers.at[layer], v_out.at[at], sems.at[at]))
        copies.append(pltpu.make_async_copy(weights.at[layer], w_out.at[at], sems.at[total + at]))
    for copy in copies:
        copy.start()
    others = clean_copies((groups, depth), slot, count, table, layers, outs, more) if count else []
    for copy in others:
        copy.start()
    shape = (rows, LANES)
    x_at = x_start + lax.broadcasted_iota(jnp.int32, shape, 0)
    lane = lax.broadcasted_iota(jnp.int32, shape, 1)
    plane = squared_dist(x_at, spacing[1], anchor[1]) + squared_dist(y_start + lane, spacing[2], anchor[2])
    flat = plane <= reach[0].astype(jnp.float32)
    for copy in copies:
        copy.wait()
    per_pack = LANES // HALO
    first = last = None
    for at in range(2 * total):
        if at < total:
            layer = table[(at // held) * depth + depth - held + at % held]
            tall = jnp.where(is_hole_layer(layer, spacing[0], anchor[0]), 1.0, 0.0)
            tile = jnp.where(flat & (jnp.full(shape, tall) > 0.5), 0.0, v_out[at])
            v_out[at] = tile
        else:
            tile = w_out[at - total]
        place = at % per_pack
        if place == 0:
            first = tile
            last = pltpu.roll(tile, HALO, 1)
        else:
            here = (lane >= HALO * place) & (lane < HALO * place + HALO)
            first = jnp.where(here, pltpu.roll(tile, HALO * place, 1), first)
            last = jnp.where(here, pltpu.roll(tile, HALO * (place + 1), 1), last)
        if place == per_pack - 1 or at == 2 * total - 1:
            first_out[at // per_pack] = first
            last_out[at // per_pack] = last
    for copy in others:
        copy.wait()


def punch(spacing, anchor, reach, layers, weights, groups, held, slot, count):
    depth = layers.shape[0] // groups
    total = groups * held
    packs = -(-2 * total // (LANES // HALO))
    tile = layers.shape[1:]
    return pl.pallas_call(
        functools.partial(punch_kernel, (groups, depth, held), slot, count),
        out_shape=[
            pltpu.VMEM((size,) + tile, jnp.float32)
            for size in [total, total, packs, packs] + ([count] * groups if count else [])
        ]
        + [TOKEN],
        in_specs=[SMEM, SMEM, SMEM, HBM, HBM],
        out_specs=[VMEM] * (5 + (groups if count else 0)),
        scratch_shapes=[
            pltpu.SMEM((groups * depth,), jnp.int32),
            pltpu.SemaphoreType.DMA((2 * total,)),
            pltpu.SemaphoreType.DMA((groups * max(1, count),)),
        ],
        compiler_params=params(),
        cost_estimate=cost(3.5),
        name="punch",
    )(spacing, anchor, reach, in_hbm(layers), in_hbm(weights))


def edge_kernel(v, w, left, right, *rest):
    top, bottom = rest[-2:]
    rows = v.shape[1]
    at = 0
    for ref in (v, w, left, right):
        count = ref.shape[0]
        top[at : at + count] = ref[:, :8]
        bottom[at : at + count] = ref[:, rows - 8 :]
        at += count


def edges(v, w, left, right, after):
    count = 2 * (v.shape[0] + left.shape[0])
    return pl.pallas_call(
        edge_kernel,
        out_shape=[jax.ShapeDtypeStruct((count, 8, LANES), jnp.float32)] * 2,
        in_specs=[VMEM] * 4 + [ANY] * len(after),
        out_specs=[VMEM] * 2,
        compiler_params=params(),
        cost_estimate=cost(0.3),
        name="edges",
    )(in_vmem(v), in_vmem(w), left, right, *after)


def fill_kernel(sizes, spacing, anchor, reach, v_in, w_in, left, right, above, below, *rest):
    groups, depth, held, full_x, full_y = sizes
    outs, (token, table, result) = rest[-groups - 3 : -3], rest[-3:]
    token[...] = jnp.zeros(token.shape, jnp.float32)
    total = groups * held
    packs = left.shape[0]
    rows = v_in.shape[1]
    me = lax.axis_index("gx")
    x_start = me * rows
    y_start = lax.axis_index("gy") * LANES
    for group in range(groups):
        order_layers(table, group * depth, group * depth, depth, spacing[0], anchor[0])
    tall = rows + 16
    shape = (tall, 2 * LANES)
    lane = lax.broadcasted_iota(jnp.int32, shape, 1)
    x_at = x_start - 8 + lax.broadcasted_iota(jnp.int32, shape, 0)
    y_at = y_start + jnp.where(lane < LANES + LANES // 2, lane, lane - 2 * LANES)
    plane = squared_dist(x_at, spacing[1], anchor[1]) + squared_dist(y_at, spacing[2], anchor[2])
    inside = (x_at >= 0) & (x_at < full_x) & (y_at >= 0) & (y_at < full_y)
    known = (lane < LANES + HALO) | (lane >= 2 * LANES - HALO)
    flat = (plane <= reach[0].astype(jnp.float32)) & inside & known
    flat_f = jnp.where(flat, 1.0, 0.0)
    per_pack = LANES // HALO
    edge_lane = lax.broadcasted_iota(jnp.int32, (tall, LANES), 1)

    def column(up, middle, down):
        return jnp.concatenate([up, middle, down], axis=0)

    def extended(ref, at, array):
        own = column(above[array], ref[at], below[array])
        pack = lax.div(array, per_pack)
        place = lax.rem(array, per_pack)
        at_left = 2 * total + pack
        at_right = 2 * total + packs + pack
        from_left = column(above[at_left], left[pack], below[at_left])
        from_right = column(above[at_right], right[pack], below[at_right])
        shift = HALO * place
        after = pltpu.roll(from_right, lax.rem(LANES - shift, LANES), 1)
        before = pltpu.roll(from_left, lax.rem(2 * LANES - HALO - shift, LANES), 1)
        edge = jnp.where(edge_lane < HALO, after, jnp.where(edge_lane >= LANES - HALO, before, 0.0))
        return jnp.concatenate([own, edge], axis=1)

    def smooth(value):
        value = pltpu.roll(value, 1, 0) + (value + value) + pltpu.roll(value, tall - 1, 0)
        return pltpu.roll(value, 1, 1) + (value + value) + pltpu.roll(value, 2 * LANES - 1, 1)

    def one(at, carry):
        layer = table[lax.div(at, held) * depth + depth - held + lax.rem(at, held)]
        hole_layer = is_hole_layer(layer, spacing[0], anchor[0])

        @pl.when(hole_layer)
        def _():
            value = extended(v_in, at, at)
            weight = extended(w_in, at, total + at)
            hole = flat_f > 0.5
            inverse = 1.0 / jnp.where(hole, smooth(weight), 1.0)
            for _ in range(3):
                value = jnp.where(hole, smooth(weight * value) * inverse, value)
            result[at] = value[8 : 8 + rows, :LANES]

        @pl.when(jnp.logical_not(hole_layer))
        def _():
            result[at] = v_in[at]

        return carry

    lax.fori_loop(0, total, one, 0)
    for k in range(groups):
        outs[k][...] = result[pl.ds((me ^ k) * held, held)]


def fill(spacing, anchor, reach, v, w, left, right, above, below, groups, held, depth, full, after):
    rows = v.shape[1]
    return pl.pallas_call(
        functools.partial(fill_kernel, (groups, depth, held) + full),
        out_shape=[jax.ShapeDtypeStruct((held, rows, LANES), jnp.float32)] * groups + [TOKEN],
        in_specs=[SMEM] * 3 + [VMEM] * 6 + [ANY] * len(after),
        out_specs=[VMEM] * (groups + 1),
        scratch_shapes=[
            pltpu.SMEM((groups * depth,), jnp.int32),
            pltpu.VMEM((groups * held, rows, LANES), jnp.float32),
        ],
        compiler_params=params(),
        cost_estimate=cost(8.5),
        name="fill",
    )(spacing, anchor, reach, in_vmem(v), in_vmem(w), left, right, above, below, *after)


def dot3(a_high, a_low, b_high, b_low, dims):
    def dot(a, b):
        return lax.dot_general(a, b, (dims, ((), ())), preferred_element_type=jnp.float32)

    return dot(a_high, b_high) + (dot(a_high, b_low) + dot(a_low, b_high))


def x_kernel(groups, step, c_high, c_low, *rest):
    pieces, (out, token, b_high, b_low) = rest[:groups], rest[-4:]
    token[...] = jnp.zeros(token.shape, jnp.float32)
    count, rows, _ = pieces[0].shape
    parts, _, out_rows, _ = out.shape
    me = lax.axis_index("gx")
    for k in range(groups):
        at = pl.ds(pl.multiple_of((me ^ k) * rows, rows), rows)
        for layer in range(count):
            high, low = split(pieces[k][layer])
            cols = pl.ds(layer * LANES, LANES)
            b_high[at, cols] = high
            b_low[at, cols] = low
    each = step // out_rows

    def some(tile, carry):
        at = pl.ds(pl.multiple_of(tile * step, step), step)
        acc = dot3(c_high[at], c_low[at], b_high[...], b_low[...], ((1,), (0,)))
        for part in range(each):
            for layer in range(count):
                out[tile * each + part, layer] = acc[
                    part * out_rows : (part + 1) * out_rows, layer * LANES : (layer + 1) * LANES
                ]
        return carry

    lax.fori_loop(0, parts // each, some, 0)


def along_x(pieces, parts, after):
    groups = len(pieces)
    count, rows, _ = pieces[0].shape
    length = rows * groups
    step = min(512, length)
    high, low = cosine_split(length)
    return pl.pallas_call(
        functools.partial(x_kernel, groups, step),
        out_shape=[pltpu.HBM((parts, count, length // parts, LANES), jnp.float32), TOKEN],
        in_specs=[VMEM] * (2 + groups) + [ANY] * len(after),
        out_specs=[VMEM, VMEM],
        scratch_shapes=[
            pltpu.VMEM((length, count * LANES), jnp.bfloat16),
            pltpu.VMEM((length, count * LANES), jnp.bfloat16),
        ],
        compiler_params=params(length),
        cost_estimate=cost(0.4 * count),
        name="along_x",
    )(high, low, *pieces, *after)


def y_kernel(slot, step, chained, spacing, anchor, c_high, c_low, pieces, *rest):
    out, token, a_high, a_low, acc, table, sems = rest[-7:]
    token[...] = jnp.zeros(token.shape, jnp.float32)
    parts, count, rows, _ = pieces.shape
    depth = out.shape[0]
    first = lax.axis_index("gx") * depth
    order_layers(table, 0, first, depth, spacing[0], anchor[0])
    for part in range(parts):
        cols = pl.ds(part * LANES, LANES)
        for layer in range(count):
            high, low = split(pieces[part, layer])
            at = pl.ds(layer * rows, rows)
            a_high[at, cols] = high
            a_low[at, cols] = low

    def copy(tile, layer):
        cols = pl.ds(pl.multiple_of(tile * step, step), step)
        return pltpu.make_async_copy(
            acc.at[tile, pl.ds(layer * rows, rows)],
            out.at[table[slot + layer] - first, :, cols],
            sems.at[tile, layer],
        )

    def some(tile, carry):
        at = pl.ds(pl.multiple_of(tile * step, step), step)
        acc[tile] = dot3(a_high[...], a_low[...], c_high[at], c_low[at], ((1,), (1,)))
        for layer in range(count):
            copy(tile, layer).start()
        return carry

    lax.fori_loop(0, acc.shape[0], some, 0)
    for tile in range(acc.shape[0]):
        for layer in range(count):
            copy(tile, layer).wait()


def along_y(spacing, anchor, pieces, slot, depth, before, after):
    parts, count, rows, _ = pieces.shape
    length = parts * LANES
    step = min(256, length)
    steps = length // step
    high, low = cosine_split(length)
    chained = before is not None
    return pl.pallas_call(
        functools.partial(y_kernel, slot, step, chained),
        out_shape=[jax.ShapeDtypeStruct((depth, rows, length), jnp.float32), TOKEN],
        in_specs=[SMEM, SMEM, VMEM, VMEM, VMEM] + ([HBM] if chained else []) + [ANY] * len(after),
        out_specs=[HBM, VMEM],
        scratch_shapes=[
            pltpu.VMEM((count * rows, length), jnp.bfloat16),
            pltpu.VMEM((count * rows, length), jnp.bfloat16),
            pltpu.VMEM((steps, count * rows, step), jnp.float32),
            pltpu.SMEM((depth,), jnp.int32),
            pltpu.SemaphoreType.DMA((steps, count)),
        ],
        input_output_aliases={5: 0} if chained else {},
        compiler_params=params(length),
        cost_estimate=cost(1.0 * count),
        name="along_y",
    )(spacing, anchor, high, low, pieces, *([before] if chained else []), *after)


def swap(value, axis, k):
    size = lax.axis_size(axis)
    return lax.ppermute(value, axis, [(i, i ^ k) for i in range(size)])


def exchange(pieces, axis):
    got = {k: swap(pieces[k], axis, k) for k in reversed(range(1, len(pieces)))}
    return [pieces[0]] + [got[k] for k in range(1, len(pieces))]


def shift(value, axis, by):
    size = lax.axis_size(axis)
    return lax.ppermute(value, axis, [(i, i + by) for i in range(size) if 0 <= i + by < size])


def per_device(intensity, weight, spacing, anchor, reach):
    layers, rows, _ = intensity.shape
    groups = lax.axis_size("gx")
    parts = lax.axis_size("gy")
    depth = layers // groups
    held = hole_slots(depth)
    full = (rows * groups, LANES * parts)

    clean = depth - held
    early = min(EARLY, clean)
    late = clean - early

    def to_rows(value):
        return lax.all_to_all(value, "gy", split_axis=0, concat_axis=0, tiled=True)

    chunks = []
    if early:
        gathered = gather_clean(spacing, anchor, intensity, groups, 0, early)
        first_pieces = exchange(gathered, "gx")
    v, w, first, last, *gathered, token = punch(
        spacing, anchor, reach, intensity, weight, groups, held, early, late
    )
    left = shift(last, "gy", 1)
    right = shift(first, "gy", -1)
    if late:
        late_pieces = exchange(gathered, "gx")
    if early:
        spectrum, token = along_x(first_pieces, parts, [left, right])
        chunks.append((0, to_rows(spectrum)))
    top, bottom = edges(v, w, left, right, [token])
    above = shift(bottom, "gx", 1)
    below = shift(top, "gx", -1)
    if late:
        spectrum, token = along_x(late_pieces, parts, [token])
        chunks.append((early, to_rows(spectrum)))
    *filled, token = fill(
        spacing, anchor, reach, v, w, left, right, above, below, groups, held, depth, full, [token]
    )
    pieces = exchange(filled, "gx")
    spectrum, token = along_x(pieces, parts, [token])
    chunks.append((clean, to_rows(spectrum)))
    out = None
    for slot, pieces in chunks:
        out, token = along_y(spacing, anchor, pieces, slot, depth, out, [token])
    return out


def solution(mesh):
    in_specs = (P(None, "gx", "gy"), P(None, "gx", "gy"), P(), P(), P())
    out_specs = P("gx", "gy", None)
    return jax.shard_map(per_device, mesh=mesh, in_specs=in_specs, out_specs=out_specs, check_vma=False)
```

```python
import functools
import math

import jax
import jax.numpy as jnp
import numpy as np
from jax import lax
from jax.experimental import pallas as pl
from jax.experimental.pallas import tpu as pltpu
from jax.sharding import PartitionSpec as P

MIN_SPACING = 10
HALO = 3
LANES = 128
PACK = LANES // (2 * HALO)
FIRST_APART = False
LAST_APART = True
EARLY = 5
HBM = pl.BlockSpec(memory_space=pltpu.HBM)
ANY = pl.BlockSpec(memory_space=pl.ANY)
SMEM = pl.BlockSpec(memory_space=pltpu.SMEM)
VMEM = pl.BlockSpec(memory_space=pltpu.VMEM)


def hole_slots(depth):
    whole, left = divmod(depth, MIN_SPACING)
    return min(depth, 3 * whole + min(3, left))


@functools.lru_cache(maxsize=None)
def cosine_split(length):
    freq = np.arange(length, dtype=np.int64)
    phase = (freq[:, None] * (2 * freq[None, :] + 1)) % (4 * length)
    matrix = np.cos(phase * (math.pi / (2 * length))) * math.sqrt(2.0 / length)
    high = matrix.astype(jnp.bfloat16)
    low = (matrix - high.astype(np.float64)).astype(jnp.bfloat16)
    return high, low


def split(value):
    high = value.astype(jnp.bfloat16)
    return high, (value - high.astype(jnp.float32)).astype(jnp.bfloat16)


def params(length=0):
    return pltpu.CompilerParams(vmem_limit_bytes=8 * 2**20 + 6 * length * length)


def cost(micros):
    return pl.CostEstimate(flops=0, bytes_accessed=int(micros * 3.6e6), transcendentals=0)


TOKEN = jax.ShapeDtypeStruct((8, LANES), jnp.float32)


def partner(n, size):
    return n if n < 3 else size + 2 - n


def in_hbm(value):
    return pltpu.with_memory_space_constraint(value, pltpu.HBM)


def in_vmem(value):
    return pltpu.with_memory_space_constraint(value, pltpu.VMEM)


def floor_mod(value, by):
    rest = lax.rem(value, by)
    return jnp.where(rest < 0, rest + by, rest)


def order_layers(table, at, first, depth, spacing, anchor):
    phase = floor_mod(first - anchor, spacing)
    front = jnp.int32(0)
    back = jnp.int32(depth - 1)
    for step in range(depth):
        hole = (phase <= 1) | (phase == spacing - 1)
        table[at + jnp.where(hole, back, front)] = first + step
        front = jnp.where(hole, front, front + 1)
        back = jnp.where(hole, back - 1, back)
        phase = jnp.where(phase + 1 == spacing, 0, phase + 1)


def is_hole_layer(layer, spacing, anchor):
    phase = floor_mod(layer - anchor, spacing)
    return (phase <= 1) | (phase == spacing - 1)


def squared_dist(position, spacing, anchor):
    step = spacing.astype(jnp.float32)
    from_anchor = (position - anchor).astype(jnp.float32)
    turns = jnp.floor((from_anchor + 0.5) / step)
    offset = from_anchor - turns * step
    dist = jnp.minimum(offset, step - offset)
    return dist * dist


def clean_copies(sizes, slot, count, table, layers, outs, sems):
    groups, depth = sizes
    me = lax.axis_index("gx")
    copies = []
    for k in range(groups):
        for part in range(count):
            layer = table[(me ^ partner(k, groups)) * depth + slot + part]
            copies.append(
                pltpu.make_async_copy(layers.at[layer], outs[k].at[part], sems.at[k * count + part])
            )
    return copies


def gather_kernel(sizes, slot, count, spacing_in, anchor_in, layers, *rest):
    groups, depth = sizes
    outs, (spacing, anchor, table, sems, small) = rest[:groups], rest[groups:]
    first = pltpu.make_async_copy(spacing_in, spacing, small.at[0])
    second = pltpu.make_async_copy(anchor_in, anchor, small.at[1])
    first.start()
    second.start()
    first.wait()
    second.wait()
    for group in range(groups):
        order_layers(table, group * depth, group * depth, depth, spacing[0], anchor[0])
    copies = clean_copies(sizes, slot, count, table, layers, outs, sems)
    for copy in copies:
        copy.start()
    for copy in copies:
        copy.wait()


def gather_clean(spacing, anchor, layers, groups, slot, count):
    depth = layers.shape[0] // groups
    return pl.pallas_call(
        functools.partial(gather_kernel, (groups, depth), slot, count),
        out_shape=[jax.ShapeDtypeStruct((count,) + layers.shape[1:], jnp.float32)] * groups,
        in_specs=[HBM] * 3,
        out_specs=[VMEM] * groups,
        scratch_shapes=[
            pltpu.SMEM(spacing.shape, jnp.int32),
            pltpu.SMEM(anchor.shape, jnp.int32),
            pltpu.SMEM((groups * depth,), jnp.int32),
            pltpu.SemaphoreType.DMA((groups * count,)),
            pltpu.SemaphoreType.DMA((2,)),
        ],
        compiler_params=params(),
        cost_estimate=cost(1.5),
        name="gather_clean",
    )(in_hbm(spacing), in_hbm(anchor), in_hbm(layers))


def punch_kernel(sizes, slot, count, spacing, anchor, reach, layers, weights, v_out, w_out, sides_out, *rest):
    groups, depth, held = sizes
    outs, (token, table, sems, more) = rest[: groups if count else 0], rest[-4:]
    token[...] = jnp.zeros(token.shape, jnp.float32)
    rows = v_out.shape[1]
    total = groups * held
    x_start = lax.axis_index("gx") * rows
    y_start = lax.axis_index("gy") * LANES
    for group in range(groups):
        order_layers(table, group * depth, group * depth, depth, spacing[0], anchor[0])
    copies = []
    for at in range(total):
        layer = table[(at // held) * depth + depth - held + at % held]
        copies.append(pltpu.make_async_copy(layers.at[layer], v_out.at[at], sems.at[at]))
        copies.append(pltpu.make_async_copy(weights.at[layer], w_out.at[at], sems.at[total + at]))
    for copy in copies:
        copy.start()
    others = clean_copies((groups, depth), slot, count, table, layers, outs, more) if count else []
    for copy in others:
        copy.start()
    shape = (rows, LANES)
    x_at = x_start + lax.broadcasted_iota(jnp.int32, shape, 0)
    lane = lax.broadcasted_iota(jnp.int32, shape, 1)
    plane = squared_dist(x_at, spacing[1], anchor[1]) + squared_dist(y_start + lane, spacing[2], anchor[2])
    flat = plane <= reach[0].astype(jnp.float32)
    for copy in copies:
        copy.wait()
    for at in range(total):
        layer = table[(at // held) * depth + depth - held + at % held]
        tall = jnp.where(is_hole_layer(layer, spacing[0], anchor[0]), 1.0, 0.0)
        v_out[at] = jnp.where(flat & (jnp.full(shape, tall) > 0.5), 0.0, v_out[at])
    for pack in range(sides_out.shape[1]):
        for kind, ref in enumerate((v_out, w_out)):
            tile = jnp.zeros(shape, jnp.float32)
            for at in range(pack * PACK, min(total, (pack + 1) * PACK)):
                place = 2 * HALO * (at % PACK)
                here = (lane >= place) & (lane < place + 2 * HALO)
                tile = jnp.where(here, pltpu.roll(ref[at], place + HALO, 1), tile)
            sides_out[kind, pack] = tile
    for copy in others:
        copy.wait()


def punch(spacing, anchor, reach, layers, weights, groups, held, slot, count):
    depth = layers.shape[0] // groups
    total = groups * held
    packs = -(-total // PACK)
    tile = layers.shape[1:]
    return pl.pallas_call(
        functools.partial(punch_kernel, (groups, depth, held), slot, count),
        out_shape=[
            pltpu.VMEM(size + tile, jnp.float32)
            for size in [(total,), (total,), (2, packs)] + ([(count,)] * groups if count else [])
        ]
        + [TOKEN],
        in_specs=[SMEM, SMEM, SMEM, HBM, HBM],
        out_specs=[VMEM] * (4 + (groups if count else 0)),
        scratch_shapes=[
            pltpu.SMEM((groups * depth,), jnp.int32),
            pltpu.SemaphoreType.DMA((2 * total,)),
            pltpu.SemaphoreType.DMA((groups * max(1, count),)),
        ],
        compiler_params=params(),
        cost_estimate=cost(3.5),
        name="punch",
    )(spacing, anchor, reach, in_hbm(layers), in_hbm(weights))


def edge_kernel(v, w, left, own, right, *rest):
    top, bottom = rest[-2:]
    rows = v.shape[1]
    at = 0
    for ref in (v, w, left, own, right):
        for array in [ref] if len(ref.shape) == 3 else [ref.at[0], ref.at[1]]:
            count = array.shape[0]
            top[at : at + count] = array[:, :8]
            bottom[at : at + count] = array[:, rows - 8 :]
            at += count


def edges(v, w, left, own, right, after):
    count = 2 * v.shape[0] + 6 * own.shape[1]
    return pl.pallas_call(
        edge_kernel,
        out_shape=[jax.ShapeDtypeStruct((count, 8, LANES), jnp.float32)] * 2,
        in_specs=[VMEM] * 5 + [ANY] * len(after),
        out_specs=[VMEM] * 2,
        compiler_params=params(),
        cost_estimate=cost(0.3),
        name="edges",
    )(in_vmem(v), in_vmem(w), left, own, right, *after)


def fill_kernel(sizes, spacing, anchor, reach, v_in, w_in, left, own, right, above, below, *rest):
    groups, depth, held, full_x, full_y = sizes
    outs, (token, table, result, beside) = rest[-groups - 4 : -4], rest[-4:]
    token[...] = jnp.zeros(token.shape, jnp.float32)
    total = groups * held
    packs = own.shape[1]
    rows = v_in.shape[1]
    me = lax.axis_index("gx")
    x_start = me * rows
    y_start = lax.axis_index("gy") * LANES
    for group in range(groups):
        order_layers(table, group * depth, group * depth, depth, spacing[0], anchor[0])
    tall = rows + 16
    shape = (tall, LANES)
    lane = lax.broadcasted_iota(jnp.int32, shape, 1)
    x_at = x_start - 8 + lax.broadcasted_iota(jnp.int32, shape, 0)
    x_dist = squared_dist(x_at, spacing[1], anchor[1])
    x_inside = (x_at >= 0) & (x_at < full_x)
    turn = jnp.floor((lane.astype(jnp.float32) + 0.5) * (0.5 / HALO))
    column = lane - 2 * HALO * turn.astype(jnp.int32)

    def holes_at(y_at):
        plane = x_dist + squared_dist(y_at, spacing[2], anchor[2])
        return (plane <= reach[0].astype(jnp.float32)) & x_inside & (y_at >= 0) & (y_at < full_y)

    def extended(ref, at, array):
        return jnp.concatenate([above[array], ref[at], below[array]], axis=0)

    def down_rows(value):
        return pltpu.roll(value, 1, 0) + (value + value) + pltpu.roll(value, tall - 1, 0)

    def lanes(value, by):
        return pltpu.roll(value, by % LANES, 1)

    def inverse_of(hole, total_weight):
        return 1.0 / jnp.where(hole, total_weight, 1.0)

    def across(value):
        return lanes(value, 1) + (value + value) + lanes(value, -1)

    inner = column < HALO
    for pack in range(packs):
        found = []
        for low, high, start in ((left, own, -HALO), (own, right, LANES - HALO)):
            tiles = []
            for kind in range(2):
                places = [
                    2 * total + (2 * {id(left): 0, id(own): 1, id(right): 2}[id(ref)] + kind) * packs + pack
                    for ref in (low, high)
                ]
                tiles.append(
                    jnp.where(
                        inner,
                        extended(low, (kind, pack), places[0]),
                        extended(high, (kind, pack), places[1]),
                    )
                )
            value, weight = tiles
            hole = holes_at(y_start + start + column)
            sums = down_rows(weight)
            kept = [sums]
            inverse = inverse_of(hole, across(sums))
            for sweep in range(3):
                sums = down_rows(weight * value)
                kept.append(sums)
                if sweep < 2:
                    value = jnp.where(hole, across(sums) * inverse, value)
            found.append(kept)
        for n in range(4):
            beside[pack, n] = jnp.where(column == HALO - 2, lanes(found[1][n], -2), found[0][n])

    flat = holes_at(y_start + lane)
    flat_f = jnp.where(flat, 1.0, 0.0)

    def one(index, carry):
        group = me ^ index
        values, weights, holes, edges_at = [], [], [], []
        for slot in range(held):
            at = group * held + slot
            layer = table[group * depth + depth - held + slot]
            swept = jnp.where(is_hole_layer(layer, spacing[0], anchor[0]), 1.0, 0.0)
            values.append(extended(v_in, at, at))
            weights.append(extended(w_in, at, total + at))
            holes.append(flat_f * swept > 0.5)
            to_edge = 2 * LANES - (2 * HALO * lax.rem(at, PACK) + HALO - 1)
            edges_at.append((lax.div(at, PACK), jnp.where(to_edge >= LANES, to_edge - LANES, to_edge)))

        def smooth(arrays, n):
            arrays = [down_rows(array) for array in arrays]
            edges = [pltpu.roll(beside[pack, n], to_edge, 1) for pack, to_edge in edges_at]
            before = [jnp.where(lane == 0, edge, lanes(array, 1)) for edge, array in zip(edges, arrays)]
            after = [jnp.where(lane == LANES - 1, edge, lanes(array, -1)) for edge, array in zip(edges, arrays)]
            return [low + (array + array) + high for low, array, high in zip(before, arrays, after)]

        inverses = [inverse_of(hole, value) for hole, value in zip(holes, smooth(weights, 0))]
        for sweep in range(3):
            sums = smooth([weight * value for weight, value in zip(weights, values)], sweep + 1)
            values = [
                jnp.where(hole, value * inverse, old)
                for hole, value, inverse, old in zip(holes, sums, inverses, values)
            ]
        for slot in range(held):
            result[index * held + slot] = values[slot][8 : 8 + rows]
        return carry

    lax.fori_loop(0, groups, one, 0)
    for n in range(groups):
        outs[n][...] = result[n * held : (n + 1) * held]


def fill(spacing, anchor, reach, v, w, sides, above, below, groups, held, depth, full, after):
    rows = v.shape[1]
    return pl.pallas_call(
        functools.partial(fill_kernel, (groups, depth, held) + full),
        out_shape=[jax.ShapeDtypeStruct((held, rows, LANES), jnp.float32)] * groups + [TOKEN],
        in_specs=[SMEM] * 3 + [VMEM] * 7 + [ANY] * len(after),
        out_specs=[VMEM] * (groups + 1),
        scratch_shapes=[
            pltpu.SMEM((groups * depth,), jnp.int32),
            pltpu.VMEM((groups * held, rows, LANES), jnp.float32),
            pltpu.VMEM((sides[0].shape[1], 4, rows + 16, LANES), jnp.float32),
        ],
        compiler_params=params(),
        cost_estimate=cost(7.0),
        name="fill",
    )(spacing, anchor, reach, in_vmem(v), in_vmem(w), *sides, above, below, *after)


def dot3(a_high, a_low, b_high, b_low, dims):
    def dot(a, b):
        return lax.dot_general(a, b, (dims, ((), ())), preferred_element_type=jnp.float32)

    return dot(a_high, b_high) + (dot(a_high, b_low) + dot(a_low, b_high))


def x_kernel(groups, made, step, c_high, c_low, *rest):
    pieces = rest[:groups]
    outs, (token, b_high, b_low, acc) = rest[-4 - made : -4], rest[-4:]
    token[...] = jnp.zeros(token.shape, jnp.float32)
    apart = len(outs) > 1
    count, rows, _ = pieces[0].shape
    out_rows = outs[0].shape[-2]
    length = c_high.shape[0]
    parts = length // out_rows
    me = lax.axis_index("gx")
    for k in range(groups):
        at = pl.ds(pl.multiple_of((me ^ partner(k, groups)) * rows, rows), rows)
        for layer in range(count):
            high, low = split(pieces[k][layer])
            cols = pl.ds(layer * LANES, LANES)
            b_high[at, cols] = high
            b_low[at, cols] = low
    each = step // out_rows

    def some(tile, carry):
        at = pl.ds(pl.multiple_of(tile * step, step), step)
        value = dot3(c_high[at], c_low[at], b_high[...], b_low[...], ((1,), (0,)))
        if apart:
            acc[at] = value
        else:
            for part in range(each):
                for layer in range(count):
                    outs[0][tile * each + part, layer] = value[
                        part * out_rows : (part + 1) * out_rows, layer * LANES : (layer + 1) * LANES
                    ]
        return carry

    lax.fori_loop(0, parts // each, some, 0)
    if apart:
        row = lax.axis_index("gy")
        for k in range(parts):
            at = pl.ds(pl.multiple_of((row ^ partner(k, parts)) * out_rows, out_rows), out_rows)
            for layer in range(count):
                outs[k][layer] = acc[at, pl.ds(layer * LANES, LANES)]


def along_x(pieces, parts, apart, after):
    groups = len(pieces)
    count, rows, _ = pieces[0].shape
    length = rows * groups
    step = min(512, length)
    high, low = cosine_split(length)
    tile = (count, length // parts, LANES)
    if apart:
        shapes = [jax.ShapeDtypeStruct(tile, jnp.float32)] * parts
    else:
        shapes = [pltpu.HBM((parts,) + tile, jnp.float32)]
    return pl.pallas_call(
        functools.partial(x_kernel, groups, len(shapes), step),
        out_shape=shapes + [TOKEN],
        in_specs=[VMEM] * (2 + groups) + [ANY] * len(after),
        out_specs=[VMEM] * (len(shapes) + 1),
        scratch_shapes=[
            pltpu.VMEM((length, count * LANES), jnp.bfloat16),
            pltpu.VMEM((length, count * LANES), jnp.bfloat16),
            pltpu.VMEM((length if apart else 8, count * LANES), jnp.float32),
        ],
        compiler_params=params(length),
        cost_estimate=cost(0.4 * count),
        name="along_x",
    )(high, low, *pieces, *after)


def column_tiles(length, step):
    return [part.T.reshape(length, -1, step).swapaxes(0, 1) for part in cosine_split(length)]


def keep_kernel(source, *rest):
    kept, token, sems = rest[-3:]
    token[...] = jnp.zeros(token.shape, jnp.float32)
    copies = [pltpu.make_async_copy(source.at[n], kept.at[n], sems.at[n]) for n in range(source.shape[0])]
    for copy in copies:
        copy.start()
    for copy in copies:
        copy.wait()


def kept_tiles(length, after):
    tiles = jnp.asarray(np.concatenate(column_tiles(length, min(256, length))))
    return pl.pallas_call(
        keep_kernel,
        out_shape=[pltpu.VMEM(tiles.shape, jnp.bfloat16), TOKEN],
        in_specs=[HBM] + [ANY] * len(after),
        out_specs=[VMEM, VMEM],
        scratch_shapes=[pltpu.SemaphoreType.DMA((tiles.shape[0],))],
        compiler_params=params(length),
        cost_estimate=cost(2.0),
        name="keep_tiles",
    )(in_hbm(tiles), *after)


def y_kernel(slot, chained, apart, spacing, anchor, cosines, *rest):
    out, token, a_high, a_low, acc, near, table, sems, more = rest[-9:]
    _, length, step = cosines.shape
    steps = length // step
    parts = length // LANES
    pieces = rest[: parts if apart else 1]
    token[...] = jnp.zeros(token.shape, jnp.float32)
    count, rows, _ = pieces[0].shape[-3:]
    depth = out.shape[0]
    if not apart:
        arrivals = [pltpu.make_async_copy(pieces[0].at[n], near.at[n], more.at[n]) for n in range(parts)]
        for arrival in arrivals:
            arrival.start()
    first = lax.axis_index("gx") * depth
    order_layers(table, 0, first, depth, spacing[0], anchor[0])
    row = lax.axis_index("gy")
    for part in range(parts):
        if apart:
            piece = pieces[part]
            cols = pl.ds(pl.multiple_of((row ^ partner(part, parts)) * LANES, LANES), LANES)
        else:
            arrivals[part].wait()
            piece = near.at[part]
            cols = pl.ds(part * LANES, LANES)
        for layer in range(count):
            high, low = split(piece[layer])
            at = pl.ds(layer * rows, rows)
            a_high[at, cols] = high
            a_low[at, cols] = low

    copies = []
    for tile in range(steps):
        acc[tile] = dot3(a_high[...], a_low[...], cosines[tile], cosines[steps + tile], ((1,), (0,)))
        for layer in range(count):
            copies.append(
                pltpu.make_async_copy(
                    acc.at[tile, pl.ds(layer * rows, rows)],
                    out.at[table[slot + layer] - first, :, pl.ds(tile * step, step)],
                    sems.at[tile, layer],
                )
            )
            copies[-1].start()
    for copy in copies:
        copy.wait()


def along_y(tiles, spacing, anchor, pieces, slot, depth, before, parts, after):
    apart = len(pieces) > 1
    count, rows, _ = pieces[0].shape[-3:]
    length = parts * LANES
    step = min(256, length)
    steps = length // step
    chained = before is not None
    near = (1, 8, LANES) if apart else pieces[0].shape[1:]
    pieces = pieces if apart else [in_hbm(pieces[0])]
    return pl.pallas_call(
        functools.partial(y_kernel, slot, chained, apart),
        out_shape=[jax.ShapeDtypeStruct((depth, rows, length), jnp.float32), TOKEN],
        in_specs=[SMEM, SMEM, VMEM]
        + [VMEM if apart else HBM] * len(pieces)
        + ([HBM] if chained else [])
        + [ANY] * len(after),
        out_specs=[HBM, VMEM],
        scratch_shapes=[
            pltpu.VMEM((count * rows, length), jnp.bfloat16),
            pltpu.VMEM((count * rows, length), jnp.bfloat16),
            pltpu.VMEM((steps, count * rows, step), jnp.float32),
            pltpu.VMEM((1 if apart else parts,) + near, jnp.float32),
            pltpu.SMEM((depth,), jnp.int32),
            pltpu.SemaphoreType.DMA((steps, count)),
            pltpu.SemaphoreType.DMA((parts,)),
        ],
        input_output_aliases={3 + len(pieces): 0} if chained else {},
        compiler_params=params(length),
        cost_estimate=cost(1.0 * count),
        name="along_y",
    )(spacing, anchor, in_vmem(tiles), *pieces, *([before] if chained else []), *after)


def swap(value, axis, k):
    size = lax.axis_size(axis)
    return lax.ppermute(value, axis, [(i, i ^ k) for i in range(size)])


def exchange(pieces, axis):
    size = len(pieces)
    return [pieces[0]] + [swap(pieces[n], axis, partner(n, size)) for n in range(1, size)]


def shift(value, axis, by):
    size = lax.axis_size(axis)
    return lax.ppermute(value, axis, [(i, i + by) for i in range(size) if 0 <= i + by < size])


def per_device(intensity, weight, spacing, anchor, reach):
    layers, rows, _ = intensity.shape
    groups = lax.axis_size("gx")
    parts = lax.axis_size("gy")
    depth = layers // groups
    held = hole_slots(depth)
    full = (rows * groups, LANES * parts)

    clean = depth - held
    early = min(EARLY, clean)
    late = clean - early

    def to_rows(spectrum, apart):
        if apart:
            return exchange(spectrum, "gy")
        return [lax.all_to_all(spectrum[0], "gy", split_axis=0, concat_axis=0, tiled=True)]

    chunks = []
    if early:
        gathered = gather_clean(spacing, anchor, intensity, groups, 0, early)
        first_pieces = exchange(gathered, "gx")
    v, w, own, *gathered, token = punch(
        spacing, anchor, reach, intensity, weight, groups, held, early, late
    )
    left = shift(own, "gy", 1)
    right = shift(own, "gy", -1)
    if late:
        late_pieces = exchange(gathered, "gx")
    if early:
        *spectrum, token = along_x(first_pieces, parts, FIRST_APART, [left, right])
        chunks.append((0, to_rows(spectrum, FIRST_APART)))
    top, bottom = edges(v, w, left, own, right, [token])
    above = shift(bottom, "gx", 1)
    below = shift(top, "gx", -1)
    *filled, token = fill(
        spacing, anchor, reach, v, w, (left, own, right), above, below, groups, held, depth, full, [token]
    )
    tiles, token = kept_tiles(full[1], [token])
    pieces = exchange([filled[partner(n, groups)] for n in range(groups)], "gx")
    *spectrum, token = along_x(pieces, parts, LAST_APART, [token])
    chunks.append((clean, to_rows(spectrum, LAST_APART)))
    out = None
    for slot, pieces in chunks:
        out, token = along_y(tiles, spacing, anchor, pieces, slot, depth, out, parts, [token])
    return out


def solution(mesh):
    in_specs = (P(None, "gx", "gy"), P(None, "gx", "gy"), P(), P(), P())
    out_specs = P("gx", "gy", None)
    return jax.shard_map(per_device, mesh=mesh, in_specs=in_specs, out_specs=out_specs, check_vma=False)
```

```python
import functools
import math

import jax
import jax.numpy as jnp
import numpy as np
from jax import lax
from jax.experimental import pallas as pl
from jax.experimental.pallas import tpu as pltpu
from jax.sharding import PartitionSpec as P

MIN_SPACING = 10
HALO = 3
LANES = 128
PACK = LANES // (2 * HALO)
FIRST_APART = False
LAST_APART = True
EARLY = 5
HBM = pl.BlockSpec(memory_space=pltpu.HBM)
ANY = pl.BlockSpec(memory_space=pl.ANY)
SMEM = pl.BlockSpec(memory_space=pltpu.SMEM)
VMEM = pl.BlockSpec(memory_space=pltpu.VMEM)


def hole_slots(depth):
    whole, left = divmod(depth, MIN_SPACING)
    return min(depth, 3 * whole + min(3, left))


@functools.lru_cache(maxsize=None)
def cosine_split(length):
    freq = np.arange(length, dtype=np.int64)
    phase = (freq[:, None] * (2 * freq[None, :] + 1)) % (4 * length)
    matrix = np.cos(phase * (math.pi / (2 * length))) * math.sqrt(2.0 / length)
    high = matrix.astype(jnp.bfloat16)
    low = (matrix - high.astype(np.float64)).astype(jnp.bfloat16)
    return high, low


def split(value):
    high = value.astype(jnp.bfloat16)
    return high, (value - high.astype(jnp.float32)).astype(jnp.bfloat16)


def params(length=0):
    return pltpu.CompilerParams(vmem_limit_bytes=8 * 2**20 + 6 * length * length)


def cost(micros):
    return pl.CostEstimate(flops=0, bytes_accessed=int(micros * 3.6e6), transcendentals=0)


TOKEN = jax.ShapeDtypeStruct((8, LANES), jnp.float32)


def partner(n, size):
    return n if n < 3 else size + 2 - n


def column_of(lane):
    turn = jnp.floor((lane.astype(jnp.float32) + 0.5) * (0.5 / HALO))
    return lane - 2 * HALO * turn.astype(jnp.int32)


def is_even(axis, shape):
    return jnp.full(shape, lax.rem(lax.axis_index(axis), 2)) == 0


def partners(size):
    return [partner(n, size) for n in range(1, size)]


def in_hbm(value):
    return pltpu.with_memory_space_constraint(value, pltpu.HBM)


def in_vmem(value):
    return pltpu.with_memory_space_constraint(value, pltpu.VMEM)


def floor_mod(value, by):
    rest = lax.rem(value, by)
    return jnp.where(rest < 0, rest + by, rest)


def order_layers(table, at, first, depth, spacing, anchor):
    phase = floor_mod(first - anchor, spacing)
    front = jnp.int32(0)
    back = jnp.int32(depth - 1)
    for step in range(depth):
        hole = (phase <= 1) | (phase == spacing - 1)
        table[at + jnp.where(hole, back, front)] = first + step
        front = jnp.where(hole, front, front + 1)
        back = jnp.where(hole, back - 1, back)
        phase = jnp.where(phase + 1 == spacing, 0, phase + 1)


def is_hole_layer(layer, spacing, anchor):
    phase = floor_mod(layer - anchor, spacing)
    return (phase <= 1) | (phase == spacing - 1)


def squared_dist(position, spacing, anchor):
    step = spacing.astype(jnp.float32)
    from_anchor = (position - anchor).astype(jnp.float32)
    turns = jnp.floor((from_anchor + 0.5) / step)
    offset = from_anchor - turns * step
    dist = jnp.minimum(offset, step - offset)
    return dist * dist


def clean_copies(depth, some, slot, count, table, layers, outs, sems):
    me = lax.axis_index("gx")
    copies = []
    for n, k in enumerate(some):
        for part in range(count):
            layer = table[(me ^ k) * depth + slot + part]
            copies.append(
                pltpu.make_async_copy(layers.at[layer], outs[n].at[part], sems.at[n * count + part])
            )
    return copies


def gather_kernel(sizes, slot, count, spacing_in, anchor_in, layers, *rest):
    groups, depth = sizes
    outs, (spacing, anchor, table, sems, small) = rest[:-5], rest[-5:]
    first = pltpu.make_async_copy(spacing_in, spacing, small.at[0])
    second = pltpu.make_async_copy(anchor_in, anchor, small.at[1])
    first.start()
    second.start()
    first.wait()
    second.wait()
    for group in range(groups):
        order_layers(table, group * depth, group * depth, depth, spacing[0], anchor[0])
    copies = clean_copies(depth, partners(groups), slot, count, table, layers, outs, sems)
    for copy in copies:
        copy.start()
    for copy in copies:
        copy.wait()


def gather_clean(spacing, anchor, layers, groups, slot, count):
    depth = layers.shape[0] // groups
    return pl.pallas_call(
        functools.partial(gather_kernel, (groups, depth), slot, count),
        out_shape=[jax.ShapeDtypeStruct((count,) + layers.shape[1:], jnp.float32)] * (groups - 1),
        in_specs=[HBM] * 3,
        out_specs=[VMEM] * (groups - 1),
        scratch_shapes=[
            pltpu.SMEM(spacing.shape, jnp.int32),
            pltpu.SMEM(anchor.shape, jnp.int32),
            pltpu.SMEM((groups * depth,), jnp.int32),
            pltpu.SemaphoreType.DMA((groups * count,)),
            pltpu.SemaphoreType.DMA((2,)),
        ],
        compiler_params=params(),
        cost_estimate=cost(1.5),
        name="gather_clean",
    )(in_hbm(spacing), in_hbm(anchor), in_hbm(layers))


def punch_kernel(sizes, early, late, spacing, anchor, reach, layers, weights, v_out, w_out, sides_out, one_out, other_out, *rest):
    groups, depth, held = sizes
    outs, (token, table, sems, more, own_sems) = rest[:-5], rest[-5:]
    token[...] = jnp.zeros(token.shape, jnp.float32)
    rows = v_out.shape[1]
    total = groups * held
    x_start = lax.axis_index("gx") * rows
    y_start = lax.axis_index("gy") * LANES
    for group in range(groups):
        order_layers(table, group * depth, group * depth, depth, spacing[0], anchor[0])
    copies = []
    for at in range(total):
        layer = table[(at // held) * depth + depth - held + at % held]
        copies.append(pltpu.make_async_copy(layers.at[layer], v_out.at[at], sems.at[at]))
        copies.append(pltpu.make_async_copy(weights.at[layer], w_out.at[at], sems.at[total + at]))
    for copy in copies:
        copy.start()
    others = []
    if early:
        others += clean_copies(depth, [0], 0, early, table, layers, outs[:1], own_sems)
        outs = outs[1:]
    if late:
        others += clean_copies(depth, range(groups), early, late, table, layers, outs, more)
    for copy in others:
        copy.start()
    shape = (rows, LANES)
    x_at = x_start + lax.broadcasted_iota(jnp.int32, shape, 0)
    lane = lax.broadcasted_iota(jnp.int32, shape, 1)
    plane = squared_dist(x_at, spacing[1], anchor[1]) + squared_dist(y_start + lane, spacing[2], anchor[2])
    flat = plane <= reach[0].astype(jnp.float32)
    for copy in copies:
        copy.wait()
    for at in range(total):
        layer = table[(at // held) * depth + depth - held + at % held]
        tall = jnp.where(is_hole_layer(layer, spacing[0], anchor[0]), 1.0, 0.0)
        v_out[at] = jnp.where(flat & (jnp.full(shape, tall) > 0.5), 0.0, v_out[at])
    for pack in range(sides_out.shape[1]):
        for kind, ref in enumerate((v_out, w_out)):
            tile = jnp.zeros(shape, jnp.float32)
            for at in range(pack * PACK, min(total, (pack + 1) * PACK)):
                place = 2 * HALO * (at % PACK)
                here = (lane >= place) & (lane < place + 2 * HALO)
                tile = jnp.where(here, pltpu.roll(ref[at], place + HALO, 1), tile)
            sides_out[kind, pack] = tile
        inner = column_of(lane) < HALO
        value, weight = sides_out[0, pack], sides_out[1, pack]
        to_right = jnp.where(inner, value, pltpu.roll(weight, HALO, 1))
        to_left = jnp.where(inner, pltpu.roll(weight, LANES - HALO, 1), value)
        even = is_even("gy", shape)
        one_out[pack] = jnp.where(even, to_right, to_left)
        other_out[pack] = jnp.where(even, to_left, to_right)
    for copy in others:
        copy.wait()


def punch(spacing, anchor, reach, layers, weights, groups, held, early, late):
    depth = layers.shape[0] // groups
    total = groups * held
    packs = -(-total // PACK)
    tile = layers.shape[1:]
    clean = ([(early,)] if early else []) + ([(late,)] * groups if late else [])
    return pl.pallas_call(
        functools.partial(punch_kernel, (groups, depth, held), early, late),
        out_shape=[
            pltpu.VMEM(size + tile, jnp.float32)
            for size in [(total,), (total,), (2, packs), (packs,), (packs,)] + clean
        ]
        + [TOKEN],
        in_specs=[SMEM, SMEM, SMEM, HBM, HBM],
        out_specs=[VMEM] * (6 + len(clean)),
        scratch_shapes=[
            pltpu.SMEM((groups * depth,), jnp.int32),
            pltpu.SemaphoreType.DMA((2 * total,)),
            pltpu.SemaphoreType.DMA((groups * max(1, late),)),
            pltpu.SemaphoreType.DMA((max(1, early),)),
        ],
        compiler_params=params(),
        cost_estimate=cost(3.5),
        name="punch",
    )(spacing, anchor, reach, in_hbm(layers), in_hbm(weights))


def edge_kernel(v, w, own, one, other, *rest):
    outs = rest[-2:]
    rows = v.shape[1]
    even = lax.rem(lax.axis_index("gx"), 2)
    for parity in range(2):

        @pl.when(even == parity)
        def _():
            bottom, top = outs if parity == 0 else outs[::-1]
            at = 0
            for ref in (v, w, own, one, other):
                for array in [ref] if len(ref.shape) == 3 else [ref.at[0], ref.at[1]]:
                    count = array.shape[0]
                    top[at : at + count] = array[:, :8]
                    bottom[at : at + count] = array[:, rows - 8 :]
                    at += count


def edges(v, w, own, one, other, after):
    count = 2 * v.shape[0] + 4 * own.shape[1]
    return pl.pallas_call(
        edge_kernel,
        out_shape=[jax.ShapeDtypeStruct((count, 8, LANES), jnp.float32)] * 2,
        in_specs=[VMEM] * 5 + [ANY] * len(after),
        out_specs=[VMEM] * 2,
        compiler_params=params(),
        cost_estimate=cost(0.3),
        name="edges",
    )(in_vmem(v), in_vmem(w), own, one, other, *after)


def fill_kernel(sizes, spacing, anchor, reach, v_in, w_in, own, one_side, other_side, one_end, other_end, *rest):
    groups, depth, held, late, full_x, full_y = sizes
    outs, (token, table, result, beside) = rest[-groups - 4 : -4], rest[-4:]
    more = rest[:groups]
    token[...] = jnp.zeros(token.shape, jnp.float32)
    total = groups * held
    packs = own.shape[1]
    rows = v_in.shape[1]
    me = lax.axis_index("gx")
    x_start = me * rows
    y_start = lax.axis_index("gy") * LANES
    for group in range(groups):
        order_layers(table, group * depth, group * depth, depth, spacing[0], anchor[0])
    tall = rows + 16
    shape = (tall, LANES)
    lane = lax.broadcasted_iota(jnp.int32, shape, 1)
    x_at = x_start - 8 + lax.broadcasted_iota(jnp.int32, shape, 0)
    x_dist = squared_dist(x_at, spacing[1], anchor[1])
    x_inside = (x_at >= 0) & (x_at < full_x)
    column = column_of(lane)

    def holes_at(y_at):
        plane = x_dist + squared_dist(y_at, spacing[2], anchor[2])
        return (plane <= reach[0].astype(jnp.float32)) & x_inside & (y_at >= 0) & (y_at < full_y)

    even_x = is_even("gx", (8, LANES))
    even_y = is_even("gy", shape)

    def extended(ref, at, array):
        one, other = one_end[array], other_end[array]
        above = jnp.where(even_x, other, one)
        below = jnp.where(even_x, one, other)
        return jnp.concatenate([above, ref[at], below], axis=0)

    def down_rows(value):
        return pltpu.roll(value, 1, 0) + (value + value) + pltpu.roll(value, tall - 1, 0)

    def lanes(value, by):
        return pltpu.roll(value, by % LANES, 1)

    def inverse_of(hole, total_weight):
        return 1.0 / jnp.where(hole, total_weight, 1.0)

    def across(value):
        return lanes(value, 1) + (value + value) + lanes(value, -1)

    inner = column < HALO
    for pack in range(packs):
        at_end = 2 * total + pack
        mine = [extended(own, (kind, pack), at_end + kind * packs) for kind in range(2)]
        one_from = extended(one_side, pack, at_end + 2 * packs)
        other_from = extended(other_side, pack, at_end + 3 * packs)
        left = jnp.where(even_y, other_from, one_from)
        right = jnp.where(even_y, one_from, other_from)
        left, right = (left, lanes(left, -HALO)), (right, lanes(right, HALO))
        found = []
        for low, high, start in ((left, mine, -HALO), (mine, right, LANES - HALO)):
            tiles = [jnp.where(inner, one, other) for one, other in zip(low, high)]
            value, weight = tiles
            hole = holes_at(y_start + start + column)
            sums = down_rows(weight)
            kept = [sums]
            inverse = inverse_of(hole, across(sums))
            for sweep in range(3):
                sums = down_rows(weight * value)
                kept.append(sums)
                if sweep < 2:
                    value = jnp.where(hole, across(sums) * inverse, value)
            found.append(kept)
        for n in range(4):
            beside[pack, n] = jnp.where(column == HALO - 2, lanes(found[1][n], -2), found[0][n])

    flat = holes_at(y_start + lane)
    flat_f = jnp.where(flat, 1.0, 0.0)

    def one(index, carry):
        group = me ^ index
        values, weights, holes, edges_at = [], [], [], []
        for slot in range(held):
            at = group * held + slot
            layer = table[group * depth + depth - held + slot]
            swept = jnp.where(is_hole_layer(layer, spacing[0], anchor[0]), 1.0, 0.0)
            values.append(extended(v_in, at, at))
            weights.append(extended(w_in, at, total + at))
            holes.append(flat_f * swept > 0.5)
            to_edge = 2 * LANES - (2 * HALO * lax.rem(at, PACK) + HALO - 1)
            edges_at.append((lax.div(at, PACK), jnp.where(to_edge >= LANES, to_edge - LANES, to_edge)))

        def smooth(arrays, n):
            arrays = [down_rows(array) for array in arrays]
            edges = [pltpu.roll(beside[pack, n], to_edge, 1) for pack, to_edge in edges_at]
            before = [jnp.where(lane == 0, edge, lanes(array, 1)) for edge, array in zip(edges, arrays)]
            after = [jnp.where(lane == LANES - 1, edge, lanes(array, -1)) for edge, array in zip(edges, arrays)]
            return [low + (array + array) + high for low, array, high in zip(before, arrays, after)]

        inverses = [inverse_of(hole, value) for hole, value in zip(holes, smooth(weights, 0))]
        for sweep in range(3):
            sums = smooth([weight * value for weight, value in zip(weights, values)], sweep + 1)
            values = [
                jnp.where(hole, value * inverse, old)
                for hole, value, inverse, old in zip(holes, sums, inverses, values)
            ]
        for slot in range(held):
            result[index * held + slot] = values[slot][8 : 8 + rows]
        return carry

    lax.fori_loop(0, groups, one, 0)
    for n in range(groups):
        if late:
            outs[n][:late] = more[n][...]
        outs[n][late:] = result[n * held : (n + 1) * held]


def fill(spacing, anchor, reach, v, w, sides, ends, late, groups, held, depth, full, after):
    count = late[0].shape[0] if late else 0
    rows = v.shape[1]
    return pl.pallas_call(
        functools.partial(fill_kernel, (groups, depth, held, count) + full),
        out_shape=[jax.ShapeDtypeStruct((count + held, rows, LANES), jnp.float32)] * groups + [TOKEN],
        in_specs=[SMEM] * 3 + [VMEM] * (7 + len(late)) + [ANY] * len(after),
        out_specs=[VMEM] * (groups + 1),
        scratch_shapes=[
            pltpu.SMEM((groups * depth,), jnp.int32),
            pltpu.VMEM((groups * held, rows, LANES), jnp.float32),
            pltpu.VMEM((sides[0].shape[1], 4, rows + 16, LANES), jnp.float32),
        ],
        compiler_params=params(),
        cost_estimate=cost(7.0),
        name="fill",
    )(spacing, anchor, reach, in_vmem(v), in_vmem(w), *sides, *ends, *late, *after)


def dot3(a_high, a_low, b_high, b_low, dims):
    def dot(a, b):
        return lax.dot_general(a, b, (dims, ((), ())), preferred_element_type=jnp.float32)

    return dot(a_high, b_high) + (dot(a_high, b_low) + dot(a_low, b_high))


def x_kernel(groups, made, step, c_high, c_low, *rest):
    pieces = rest[:groups]
    outs, (token, b_high, b_low, acc, sems) = rest[-5 - made : -5], rest[-5:]
    token[...] = jnp.zeros(token.shape, jnp.float32)
    apart = len(outs) > 1
    count, rows, _ = pieces[0].shape
    out_rows = outs[0].shape[-2]
    length = c_high.shape[0]
    parts = length // out_rows
    me = lax.axis_index("gx")
    for k in range(groups):
        at = pl.ds(pl.multiple_of((me ^ partner(k, groups)) * rows, rows), rows)
        for layer in range(count):
            high, low = split(pieces[k][layer])
            cols = pl.ds(layer * LANES, LANES)
            b_high[at, cols] = high
            b_low[at, cols] = low
    each = step // out_rows
    copies = []
    for tile in range(length // step):
        at = pl.ds(tile * step, step)
        value = dot3(c_high[at], c_low[at], b_high[...], b_low[...], ((1,), (0,)))
        if apart:
            acc[at] = value
            continue
        for part in range(each):
            for layer in range(count):
                acc[tile * each + part, layer] = value[
                    part * out_rows : (part + 1) * out_rows, layer * LANES : (layer + 1) * LANES
                ]
        some = pl.ds(tile * each, each)
        copies.append(pltpu.make_async_copy(acc.at[some], outs[0].at[some], sems.at[tile]))
        copies[-1].start()
    for copy in copies:
        copy.wait()
    if apart:
        row = lax.axis_index("gy")
        for k in range(parts):
            at = pl.ds(pl.multiple_of((row ^ partner(k, parts)) * out_rows, out_rows), out_rows)
            for layer in range(count):
                outs[k][layer] = acc[at, pl.ds(layer * LANES, LANES)]


def along_x(pieces, parts, apart, after):
    groups = len(pieces)
    count, rows, _ = pieces[0].shape
    length = rows * groups
    step = min(512 if apart else 256, length)
    high, low = cosine_split(length)
    tile = (count, length // parts, LANES)
    if apart:
        shapes = [jax.ShapeDtypeStruct(tile, jnp.float32)] * parts
    else:
        shapes = [pltpu.HBM((parts,) + tile, jnp.float32)]
    return pl.pallas_call(
        functools.partial(x_kernel, groups, len(shapes), step),
        out_shape=shapes + [TOKEN],
        in_specs=[VMEM] * (2 + groups) + [ANY] * len(after),
        out_specs=[VMEM if apart else HBM] * len(shapes) + [VMEM],
        scratch_shapes=[
            pltpu.VMEM((length, count * LANES), jnp.bfloat16),
            pltpu.VMEM((length, count * LANES), jnp.bfloat16),
            pltpu.VMEM((length, count * LANES) if apart else (parts,) + tile, jnp.float32),
            pltpu.SemaphoreType.DMA((length // step,)),
        ],
        compiler_params=params(length),
        cost_estimate=cost(0.4 * count),
        name="along_x",
    )(high, low, *pieces, *after)


def column_tiles(length, step):
    return [part.T.reshape(length, -1, step).swapaxes(0, 1) for part in cosine_split(length)]


def keep_kernel(source, *rest):
    kept, token, sems = rest[-3:]
    token[...] = jnp.zeros(token.shape, jnp.float32)
    copies = [pltpu.make_async_copy(source.at[n], kept.at[n], sems.at[n]) for n in range(source.shape[0])]
    for copy in copies:
        copy.start()
    for copy in copies:
        copy.wait()


def kept_tiles(length, after):
    tiles = jnp.asarray(np.concatenate(column_tiles(length, min(256, length))))
    return pl.pallas_call(
        keep_kernel,
        out_shape=[pltpu.VMEM(tiles.shape, jnp.bfloat16), TOKEN],
        in_specs=[HBM] + [ANY] * len(after),
        out_specs=[VMEM, VMEM],
        scratch_shapes=[pltpu.SemaphoreType.DMA((tiles.shape[0],))],
        compiler_params=params(length),
        cost_estimate=cost(2.0),
        name="keep_tiles",
    )(in_hbm(tiles), *after)


def y_kernel(slot, chained, apart, spacing, anchor, cosines, *rest):
    out, token, a_high, a_low, acc, near, table, sems, more = rest[-9:]
    _, length, step = cosines.shape
    steps = length // step
    parts = length // LANES
    pieces = rest[: parts if apart else 1]
    token[...] = jnp.zeros(token.shape, jnp.float32)
    count, rows, _ = pieces[0].shape[-3:]
    depth = out.shape[0]
    if not apart:
        arrivals = [pltpu.make_async_copy(pieces[0].at[n], near.at[n], more.at[n]) for n in range(parts)]
        for arrival in arrivals:
            arrival.start()
    first = lax.axis_index("gx") * depth
    order_layers(table, 0, first, depth, spacing[0], anchor[0])
    row = lax.axis_index("gy")
    for part in range(parts):
        if apart:
            piece = pieces[part]
            cols = pl.ds(pl.multiple_of((row ^ partner(part, parts)) * LANES, LANES), LANES)
        else:
            arrivals[part].wait()
            piece = near.at[part]
            cols = pl.ds(part * LANES, LANES)
        for layer in range(count):
            high, low = split(piece[layer])
            at = pl.ds(layer * rows, rows)
            a_high[at, cols] = high
            a_low[at, cols] = low

    copies = []
    for tile in range(steps):
        acc[tile] = dot3(a_high[...], a_low[...], cosines[tile], cosines[steps + tile], ((1,), (0,)))
        for layer in range(count):
            copies.append(
                pltpu.make_async_copy(
                    acc.at[tile, pl.ds(layer * rows, rows)],
                    out.at[table[slot + layer] - first, :, pl.ds(tile * step, step)],
                    sems.at[tile, layer],
                )
            )
            copies[-1].start()
    for copy in copies:
        copy.wait()


def along_y(tiles, spacing, anchor, pieces, slot, depth, before, parts, after):
    apart = len(pieces) > 1
    count, rows, _ = pieces[0].shape[-3:]
    length = parts * LANES
    step = min(256, length)
    steps = length // step
    chained = before is not None
    near = (1, 8, LANES) if apart else pieces[0].shape[1:]
    pieces = pieces if apart else [in_hbm(pieces[0])]
    return pl.pallas_call(
        functools.partial(y_kernel, slot, chained, apart),
        out_shape=[jax.ShapeDtypeStruct((depth, rows, length), jnp.float32), TOKEN],
        in_specs=[SMEM, SMEM, VMEM]
        + [VMEM if apart else HBM] * len(pieces)
        + ([HBM] if chained else [])
        + [ANY] * len(after),
        out_specs=[HBM, VMEM],
        scratch_shapes=[
            pltpu.VMEM((count * rows, length), jnp.bfloat16),
            pltpu.VMEM((count * rows, length), jnp.bfloat16),
            pltpu.VMEM((steps, count * rows, step), jnp.float32),
            pltpu.VMEM((1 if apart else parts,) + near, jnp.float32),
            pltpu.SMEM((depth,), jnp.int32),
            pltpu.SemaphoreType.DMA((steps, count)),
            pltpu.SemaphoreType.DMA((parts,)),
        ],
        input_output_aliases={3 + len(pieces): 0} if chained else {},
        compiler_params=params(length),
        cost_estimate=cost(1.0 * count),
        name="along_y",
    )(spacing, anchor, in_vmem(tiles), *pieces, *([before] if chained else []), *after)


def swap(value, axis, k):
    size = lax.axis_size(axis)
    return lax.ppermute(value, axis, [(i, i ^ k) for i in range(size)])


def exchange(pieces, axis):
    return [swap(piece, axis, k) for piece, k in zip(pieces, partners(len(pieces) + 1))]


def swap_neighbours(first, second, axis):
    size = lax.axis_size(axis)
    answers = []
    for value, start in ((first, 0), (second, 1)):
        pairs = [(i, i + 1) for i in range(start, size - 1, 2)]
        answers.append(lax.ppermute(value, axis, pairs + [(j, i) for i, j in pairs]))
    return answers


def per_device(intensity, weight, spacing, anchor, reach):
    layers, rows, _ = intensity.shape
    groups = lax.axis_size("gx")
    parts = lax.axis_size("gy")
    depth = layers // groups
    held = hole_slots(depth)
    full = (rows * groups, LANES * parts)

    clean = depth - held
    early = min(EARLY, clean)
    late = clean - early

    def to_rows(spectrum, apart):
        if apart:
            return spectrum[:1] + exchange(spectrum[1:], "gy")
        return [lax.all_to_all(spectrum[0], "gy", split_axis=0, concat_axis=0, tiled=True)]

    chunks = []
    if early:
        gathered = gather_clean(spacing, anchor, intensity, groups, 0, early)
        first_pieces = exchange(gathered, "gx")
    v, w, own, one, other, *mine, token = punch(
        spacing, anchor, reach, intensity, weight, groups, held, early, late
    )
    sides = swap_neighbours(one, other, "gy")
    ends = swap_neighbours(*edges(v, w, own, *sides, []), "gx")
    if early:
        first_pieces = mine[:1] + first_pieces
        mine = mine[1:]
        *spectrum, token = along_x(first_pieces, parts, FIRST_APART, sides)
        chunks.append((0, to_rows(spectrum, FIRST_APART)))
    *filled, token = fill(
        spacing, anchor, reach, v, w, [own] + sides, ends, mine, groups, held, depth, full, [token]
    )
    tiles, token = kept_tiles(full[1], [token])
    pieces = filled[:1] + exchange([filled[k] for k in partners(groups)], "gx")
    *spectrum, token = along_x(pieces, parts, LAST_APART, [token])
    chunks.append((early, to_rows(spectrum, LAST_APART)))
    out = None
    for slot, pieces in chunks:
        out, token = along_y(tiles, spacing, anchor, pieces, slot, depth, out, parts, [token])
    return out


def solution(mesh):
    in_specs = (P(None, "gx", "gy"), P(None, "gx", "gy"), P(), P(), P())
    out_specs = P("gx", "gy", None)
    return jax.shard_map(per_device, mesh=mesh, in_specs=in_specs, out_specs=out_specs, check_vma=False)
```

```python
import functools
import math

import jax
import jax.numpy as jnp
import numpy as np
from jax import lax
from jax.experimental import pallas as pl
from jax.experimental.pallas import tpu as pltpu
from jax.sharding import PartitionSpec as P

MIN_SPACING = 10
HALO = 3
LANES = 128
PACK = LANES // (2 * HALO)
FIRST_APART = False
LAST_APART = True
EARLY = 5
HBM = pl.BlockSpec(memory_space=pltpu.HBM)
ANY = pl.BlockSpec(memory_space=pl.ANY)
SMEM = pl.BlockSpec(memory_space=pltpu.SMEM)
VMEM = pl.BlockSpec(memory_space=pltpu.VMEM)


def hole_slots(depth):
    whole, left = divmod(depth, MIN_SPACING)
    return min(depth, 3 * whole + min(3, left))


@functools.lru_cache(maxsize=None)
def cosine_split(length):
    freq = np.arange(length, dtype=np.int64)
    phase = (freq[:, None] * (2 * freq[None, :] + 1)) % (4 * length)
    matrix = np.cos(phase * (math.pi / (2 * length))) * math.sqrt(2.0 / length)
    high = matrix.astype(jnp.bfloat16)
    low = (matrix - high.astype(np.float64)).astype(jnp.bfloat16)
    return high, low


def split(value):
    high = value.astype(jnp.bfloat16)
    return high, (value - high.astype(jnp.float32)).astype(jnp.bfloat16)


def params(length=0):
    return pltpu.CompilerParams(vmem_limit_bytes=8 * 2**20 + 6 * length * length)


def cost(micros):
    return pl.CostEstimate(flops=0, bytes_accessed=int(micros * 3.6e6), transcendentals=0)


TOKEN = jax.ShapeDtypeStruct((8, LANES), jnp.float32)


def partner(n, size):
    return n if n < 4 else size + 3 - n


def column_of(lane):
    turn = jnp.floor((lane.astype(jnp.float32) + 0.5) * (0.5 / HALO))
    return lane - 2 * HALO * turn.astype(jnp.int32)


def is_even(axis, shape):
    return jnp.full(shape, lax.rem(lax.axis_index(axis), 2)) == 0


def early_pieces(parts):
    return parts // 2 + 1


def partners(size):
    return [partner(n, size) for n in range(1, size)]


def in_hbm(value):
    return pltpu.with_memory_space_constraint(value, pltpu.HBM)


def in_vmem(value):
    return pltpu.with_memory_space_constraint(value, pltpu.VMEM)


def floor_mod(value, by):
    rest = lax.rem(value, by)
    return jnp.where(rest < 0, rest + by, rest)


def order_layers(table, at, first, depth, spacing, anchor):
    phase = floor_mod(first - anchor, spacing)
    front = jnp.int32(0)
    back = jnp.int32(depth - 1)
    for step in range(depth):
        hole = (phase <= 1) | (phase == spacing - 1)
        table[at + jnp.where(hole, back, front)] = first + step
        front = jnp.where(hole, front, front + 1)
        back = jnp.where(hole, back - 1, back)
        phase = jnp.where(phase + 1 == spacing, 0, phase + 1)


def is_hole_layer(layer, spacing, anchor):
    phase = floor_mod(layer - anchor, spacing)
    return (phase <= 1) | (phase == spacing - 1)


def squared_dist(position, spacing, anchor):
    step = spacing.astype(jnp.float32)
    from_anchor = (position - anchor).astype(jnp.float32)
    turns = jnp.floor((from_anchor + 0.5) / step)
    offset = from_anchor - turns * step
    dist = jnp.minimum(offset, step - offset)
    return dist * dist


def clean_copies(depth, some, slot, count, table, layers, outs, sems):
    me = lax.axis_index("gx")
    copies = []
    for n, k in enumerate(some):
        for part in range(count):
            layer = table[(me ^ k) * depth + slot + part]
            copies.append(
                pltpu.make_async_copy(layers.at[layer], outs[n].at[part], sems.at[n * count + part])
            )
    return copies


def gather_kernel(sizes, slot, count, spacing_in, anchor_in, layers, *rest):
    groups, depth = sizes
    outs, (spacing, anchor, table, sems, small) = rest[:-5], rest[-5:]
    first = pltpu.make_async_copy(spacing_in, spacing, small.at[0])
    second = pltpu.make_async_copy(anchor_in, anchor, small.at[1])
    first.start()
    second.start()
    first.wait()
    second.wait()
    for group in range(groups):
        order_layers(table, group * depth, group * depth, depth, spacing[0], anchor[0])
    copies = clean_copies(depth, partners(groups), slot, count, table, layers, outs, sems)
    for copy in copies:
        copy.start()
    for copy in copies:
        copy.wait()


def gather_clean(spacing, anchor, layers, groups, slot, count):
    depth = layers.shape[0] // groups
    return pl.pallas_call(
        functools.partial(gather_kernel, (groups, depth), slot, count),
        out_shape=[jax.ShapeDtypeStruct((count,) + layers.shape[1:], jnp.float32)] * (groups - 1),
        in_specs=[HBM] * 3,
        out_specs=[VMEM] * (groups - 1),
        scratch_shapes=[
            pltpu.SMEM(spacing.shape, jnp.int32),
            pltpu.SMEM(anchor.shape, jnp.int32),
            pltpu.SMEM((groups * depth,), jnp.int32),
            pltpu.SemaphoreType.DMA((groups * count,)),
            pltpu.SemaphoreType.DMA((2,)),
        ],
        compiler_params=params(),
        cost_estimate=cost(1.5),
        name="gather_clean",
    )(in_hbm(spacing), in_hbm(anchor), in_hbm(layers))


def punch_kernel(sizes, early, late, spacing, anchor, reach, layers, weights, v_out, w_out, sides_out, one_out, other_out, *rest):
    groups, depth, held = sizes
    outs, (token, table, sems, more, own_sems) = rest[:-5], rest[-5:]
    token[...] = jnp.zeros(token.shape, jnp.float32)
    rows = v_out.shape[1]
    total = groups * held
    x_start = lax.axis_index("gx") * rows
    y_start = lax.axis_index("gy") * LANES
    for group in range(groups):
        order_layers(table, group * depth, group * depth, depth, spacing[0], anchor[0])
    copies = []
    for at in range(total):
        layer = table[(at // held) * depth + depth - held + at % held]
        copies.append(pltpu.make_async_copy(layers.at[layer], v_out.at[at], sems.at[at]))
        copies.append(pltpu.make_async_copy(weights.at[layer], w_out.at[at], sems.at[total + at]))
    for copy in copies:
        copy.start()
    others = []
    if early:
        others += clean_copies(depth, [0], 0, early, table, layers, outs[:1], own_sems)
        outs = outs[1:]
    if late:
        others += clean_copies(depth, range(groups), early, late, table, layers, outs, more)
    for copy in others:
        copy.start()
    shape = (rows, LANES)
    x_at = x_start + lax.broadcasted_iota(jnp.int32, shape, 0)
    lane = lax.broadcasted_iota(jnp.int32, shape, 1)
    plane = squared_dist(x_at, spacing[1], anchor[1]) + squared_dist(y_start + lane, spacing[2], anchor[2])
    flat = plane <= reach[0].astype(jnp.float32)
    for copy in copies:
        copy.wait()
    for at in range(total):
        layer = table[(at // held) * depth + depth - held + at % held]
        tall = jnp.where(is_hole_layer(layer, spacing[0], anchor[0]), 1.0, 0.0)
        v_out[at] = jnp.where(flat & (jnp.full(shape, tall) > 0.5), 0.0, v_out[at])
    for pack in range(sides_out.shape[1]):
        for kind, ref in enumerate((v_out, w_out)):
            tile = jnp.zeros(shape, jnp.float32)
            for at in range(pack * PACK, min(total, (pack + 1) * PACK)):
                place = 2 * HALO * (at % PACK)
                here = (lane >= place) & (lane < place + 2 * HALO)
                tile = jnp.where(here, pltpu.roll(ref[at], place + HALO, 1), tile)
            sides_out[kind, pack] = tile
        inner = column_of(lane) < HALO
        value, weight = sides_out[0, pack], sides_out[1, pack]
        to_right = jnp.where(inner, value, pltpu.roll(weight, HALO, 1))
        to_left = jnp.where(inner, pltpu.roll(weight, LANES - HALO, 1), value)
        even = is_even("gy", shape)
        one_out[pack] = jnp.where(even, to_right, to_left)
        other_out[pack] = jnp.where(even, to_left, to_right)
    for copy in others:
        copy.wait()


def punch(spacing, anchor, reach, layers, weights, groups, held, early, late):
    depth = layers.shape[0] // groups
    total = groups * held
    packs = -(-total // PACK)
    tile = layers.shape[1:]
    clean = ([(early,)] if early else []) + ([(late,)] * groups if late else [])
    return pl.pallas_call(
        functools.partial(punch_kernel, (groups, depth, held), early, late),
        out_shape=[
            pltpu.VMEM(size + tile, jnp.float32)
            for size in [(total,), (total,), (2, packs), (packs,), (packs,)] + clean
        ]
        + [TOKEN],
        in_specs=[SMEM, SMEM, SMEM, HBM, HBM],
        out_specs=[VMEM] * (6 + len(clean)),
        scratch_shapes=[
            pltpu.SMEM((groups * depth,), jnp.int32),
            pltpu.SemaphoreType.DMA((2 * total,)),
            pltpu.SemaphoreType.DMA((groups * max(1, late),)),
            pltpu.SemaphoreType.DMA((max(1, early),)),
        ],
        compiler_params=params(),
        cost_estimate=cost(3.5),
        name="punch",
    )(spacing, anchor, reach, in_hbm(layers), in_hbm(weights))


def edge_kernel(v, w, own, one, other, *rest):
    outs = rest[-2:]
    rows = v.shape[1]
    even = lax.rem(lax.axis_index("gx"), 2)
    for parity in range(2):

        @pl.when(even == parity)
        def _():
            bottom, top = outs if parity == 0 else outs[::-1]
            at = 0
            for ref in (v, w, own, one, other):
                for array in [ref] if len(ref.shape) == 3 else [ref.at[0], ref.at[1]]:
                    count = array.shape[0]
                    top[at : at + count] = array[:, :8]
                    bottom[at : at + count] = array[:, rows - 8 :]
                    at += count


def edges(v, w, own, one, other, after):
    count = 2 * v.shape[0] + 4 * own.shape[1]
    return pl.pallas_call(
        edge_kernel,
        out_shape=[jax.ShapeDtypeStruct((count, 8, LANES), jnp.float32)] * 2,
        in_specs=[VMEM] * 5 + [ANY] * len(after),
        out_specs=[VMEM] * 2,
        compiler_params=params(),
        cost_estimate=cost(0.3),
        name="edges",
    )(in_vmem(v), in_vmem(w), own, one, other, *after)


def fill_kernel(sizes, spacing, anchor, reach, v_in, w_in, own, one_side, other_side, one_end, other_end, *rest):
    groups, depth, held, late, full_x, full_y = sizes
    outs, (token, table, result, beside) = rest[-groups - 4 : -4], rest[-4:]
    more = rest[:groups]
    token[...] = jnp.zeros(token.shape, jnp.float32)
    total = groups * held
    packs = own.shape[1]
    rows = v_in.shape[1]
    me = lax.axis_index("gx")
    x_start = me * rows
    y_start = lax.axis_index("gy") * LANES
    for group in range(groups):
        order_layers(table, group * depth, group * depth, depth, spacing[0], anchor[0])
    tall = rows + 16
    shape = (tall, LANES)
    lane = lax.broadcasted_iota(jnp.int32, shape, 1)
    x_at = x_start - 8 + lax.broadcasted_iota(jnp.int32, shape, 0)
    x_dist = squared_dist(x_at, spacing[1], anchor[1])
    x_inside = (x_at >= 0) & (x_at < full_x)
    column = column_of(lane)

    def holes_at(y_at):
        plane = x_dist + squared_dist(y_at, spacing[2], anchor[2])
        return (plane <= reach[0].astype(jnp.float32)) & x_inside & (y_at >= 0) & (y_at < full_y)

    even_x = is_even("gx", (8, LANES))
    even_y = is_even("gy", shape)

    def extended(ref, at, array):
        one, other = one_end[array], other_end[array]
        above = jnp.where(even_x, other, one)
        below = jnp.where(even_x, one, other)
        return jnp.concatenate([above, ref[at], below], axis=0)

    def down_rows(value):
        return pltpu.roll(value, 1, 0) + (value + value) + pltpu.roll(value, tall - 1, 0)

    def lanes(value, by):
        return pltpu.roll(value, by % LANES, 1)

    def inverse_of(hole, total_weight):
        return 1.0 / jnp.where(hole, total_weight, 1.0)

    def across(value):
        return lanes(value, 1) + (value + value) + lanes(value, -1)

    inner = column < HALO
    for pack in range(packs):
        at_end = 2 * total + pack
        mine = [extended(own, (kind, pack), at_end + kind * packs) for kind in range(2)]
        one_from = extended(one_side, pack, at_end + 2 * packs)
        other_from = extended(other_side, pack, at_end + 3 * packs)
        left = jnp.where(even_y, other_from, one_from)
        right = jnp.where(even_y, one_from, other_from)
        left, right = (left, lanes(left, -HALO)), (right, lanes(right, HALO))
        found = []
        for low, high, start in ((left, mine, -HALO), (mine, right, LANES - HALO)):
            tiles = [jnp.where(inner, one, other) for one, other in zip(low, high)]
            value, weight = tiles
            hole = holes_at(y_start + start + column)
            sums = down_rows(weight)
            kept = [sums]
            inverse = inverse_of(hole, across(sums))
            for sweep in range(3):
                sums = down_rows(weight * value)
                kept.append(sums)
                if sweep < 2:
                    value = jnp.where(hole, across(sums) * inverse, value)
            found.append(kept)
        for n in range(4):
            beside[pack, n] = jnp.where(column == HALO - 2, lanes(found[1][n], -2), found[0][n])

    flat = holes_at(y_start + lane)
    flat_f = jnp.where(flat, 1.0, 0.0)

    def one(index, carry):
        group = me ^ index
        values, weights, holes, edges_at = [], [], [], []
        for slot in range(held):
            at = group * held + slot
            layer = table[group * depth + depth - held + slot]
            swept = jnp.where(is_hole_layer(layer, spacing[0], anchor[0]), 1.0, 0.0)
            values.append(extended(v_in, at, at))
            weights.append(extended(w_in, at, total + at))
            holes.append(flat_f * swept > 0.5)
            to_edge = 2 * LANES - (2 * HALO * lax.rem(at, PACK) + HALO - 1)
            edges_at.append((lax.div(at, PACK), jnp.where(to_edge >= LANES, to_edge - LANES, to_edge)))

        def smooth(arrays, n):
            arrays = [down_rows(array) for array in arrays]
            edges = [pltpu.roll(beside[pack, n], to_edge, 1) for pack, to_edge in edges_at]
            before = [jnp.where(lane == 0, edge, lanes(array, 1)) for edge, array in zip(edges, arrays)]
            after = [jnp.where(lane == LANES - 1, edge, lanes(array, -1)) for edge, array in zip(edges, arrays)]
            return [low + (array + array) + high for low, array, high in zip(before, arrays, after)]

        inverses = [inverse_of(hole, value) for hole, value in zip(holes, smooth(weights, 0))]
        for sweep in range(3):
            sums = smooth([weight * value for weight, value in zip(weights, values)], sweep + 1)
            values = [
                jnp.where(hole, value * inverse, old)
                for hole, value, inverse, old in zip(holes, sums, inverses, values)
            ]
        for slot in range(held):
            result[index * held + slot] = values[slot][8 : 8 + rows]
        return carry

    lax.fori_loop(0, groups, one, 0)
    for n in range(groups):
        if late:
            outs[n][:late] = more[n][...]
        outs[n][late:] = result[n * held : (n + 1) * held]


def fill(spacing, anchor, reach, v, w, sides, ends, late, groups, held, depth, full, after):
    count = late[0].shape[0] if late else 0
    rows = v.shape[1]
    return pl.pallas_call(
        functools.partial(fill_kernel, (groups, depth, held, count) + full),
        out_shape=[jax.ShapeDtypeStruct((count + held, rows, LANES), jnp.float32)] * groups + [TOKEN],
        in_specs=[SMEM] * 3 + [VMEM] * (7 + len(late)) + [ANY] * len(after),
        out_specs=[VMEM] * (groups + 1),
        scratch_shapes=[
            pltpu.SMEM((groups * depth,), jnp.int32),
            pltpu.VMEM((groups * held, rows, LANES), jnp.float32),
            pltpu.VMEM((sides[0].shape[1], 4, rows + 16, LANES), jnp.float32),
        ],
        compiler_params=params(),
        cost_estimate=cost(7.0),
        name="fill",
    )(spacing, anchor, reach, in_vmem(v), in_vmem(w), *sides, *ends, *late, *after)


def dot3(a_high, a_low, b_high, b_low, dims):
    def dot(a, b):
        return lax.dot_general(a, b, (dims, ((), ())), preferred_element_type=jnp.float32)

    return dot(a_high, b_high) + (dot(a_high, b_low) + dot(a_low, b_high))


def x_kernel(groups, made, step, c_high, c_low, *rest):
    pieces = rest[:groups]
    outs, (token, b_high, b_low, acc, sems) = rest[-5 - made : -5], rest[-5:]
    token[...] = jnp.zeros(token.shape, jnp.float32)
    apart = len(outs) > 1
    count, rows, _ = pieces[0].shape
    out_rows = outs[0].shape[-2]
    length = c_high.shape[0]
    parts = length // out_rows
    me = lax.axis_index("gx")
    for k in range(groups):
        at = pl.ds(pl.multiple_of((me ^ partner(k, groups)) * rows, rows), rows)
        for layer in range(count):
            high, low = split(pieces[k][layer])
            cols = pl.ds(layer * LANES, LANES)
            b_high[at, cols] = high
            b_low[at, cols] = low
    each = step // out_rows
    copies = []
    for tile in range(length // step):
        at = pl.ds(tile * step, step)
        value = dot3(c_high[at], c_low[at], b_high[...], b_low[...], ((1,), (0,)))
        if apart:
            acc[at] = value
            continue
        for part in range(each):
            for layer in range(count):
                acc[tile * each + part, layer] = value[
                    part * out_rows : (part + 1) * out_rows, layer * LANES : (layer + 1) * LANES
                ]
        some = pl.ds(tile * each, each)
        copies.append(pltpu.make_async_copy(acc.at[some], outs[0].at[some], sems.at[tile]))
        copies[-1].start()
    for copy in copies:
        copy.wait()
    if apart:
        row = lax.axis_index("gy")
        for k in range(parts):
            at = pl.ds(pl.multiple_of((row ^ partner(k, parts)) * out_rows, out_rows), out_rows)
            for layer in range(count):
                outs[k][layer] = acc[at, pl.ds(layer * LANES, LANES)]


def along_x(pieces, parts, apart, after):
    groups = len(pieces)
    count, rows, _ = pieces[0].shape
    length = rows * groups
    step = min(512 if apart else 256, length)
    high, low = cosine_split(length)
    tile = (count, length // parts, LANES)
    if apart:
        shapes = [jax.ShapeDtypeStruct(tile, jnp.float32)] * parts
    else:
        shapes = [pltpu.HBM((parts,) + tile, jnp.float32)]
    return pl.pallas_call(
        functools.partial(x_kernel, groups, len(shapes), step),
        out_shape=shapes + [TOKEN],
        in_specs=[VMEM] * (2 + groups) + [ANY] * len(after),
        out_specs=[VMEM if apart else HBM] * len(shapes) + [VMEM],
        scratch_shapes=[
            pltpu.VMEM((length, count * LANES), jnp.bfloat16),
            pltpu.VMEM((length, count * LANES), jnp.bfloat16),
            pltpu.VMEM((length, count * LANES) if apart else (parts,) + tile, jnp.float32),
            pltpu.SemaphoreType.DMA((length // step,)),
        ],
        compiler_params=params(length),
        cost_estimate=cost(0.4 * count),
        name="along_x",
    )(high, low, *pieces, *after)


def column_tiles(length, step):
    return [part.T.reshape(length, -1, step).swapaxes(0, 1) for part in cosine_split(length)]


def y_part_kernel(parts, cosines, *rest):
    out, a_high, a_low = rest[-3:]
    steps = out.shape[0]
    early = early_pieces(parts)
    pieces = rest[:early]
    count, rows, _ = pieces[0].shape
    row = lax.axis_index("gy")
    for n in range(parts):
        cols = pl.ds(pl.multiple_of((row ^ partner(n, parts)) * LANES, LANES), LANES)
        for layer in range(count):
            at = pl.ds(layer * rows, rows)
            if n < early:
                a_high[at, cols], a_low[at, cols] = split(pieces[n][layer])
            else:
                a_high[at, cols] = jnp.zeros((rows, LANES), jnp.bfloat16)
                a_low[at, cols] = jnp.zeros((rows, LANES), jnp.bfloat16)
    for tile in range(steps):
        out[tile] = dot3(a_high[...], a_low[...], cosines[tile], cosines[steps + tile], ((1,), (0,)))


def along_y_part(tiles, pieces, parts, after):
    count, rows, _ = pieces[0].shape
    _, length, step = tiles.shape
    return pl.pallas_call(
        functools.partial(y_part_kernel, parts),
        out_shape=jax.ShapeDtypeStruct((length // step, count * rows, step), jnp.float32),
        in_specs=[VMEM] * (1 + len(pieces)) + [ANY] * len(after),
        out_specs=VMEM,
        scratch_shapes=[pltpu.VMEM((count * rows, length), jnp.bfloat16)] * 2,
        compiler_params=params(length),
        cost_estimate=cost(2.0),
        name="along_y_part",
    )(in_vmem(tiles), *pieces, *after)


def y_rest_kernel(parts, slot, chained, spacing, anchor, cosines, partial, *rest):
    out, acc, table, sems = rest[-4:]
    early = early_pieces(parts)
    pieces = rest[: parts - early]
    steps = partial.shape[0]
    step = partial.shape[2]
    count, rows, _ = pieces[0].shape
    depth = out.shape[0]
    first = lax.axis_index("gx") * depth
    order_layers(table, 0, first, depth, spacing[0], anchor[0])
    row = lax.axis_index("gy")
    halves, places = [], []
    for n, piece in enumerate(pieces):
        halves.append(split(jnp.concatenate([piece[layer] for layer in range(count)], axis=0)))
        start = (row ^ partner(early + n, parts)) * LANES
        places.append(pl.ds(pl.multiple_of(start, LANES), LANES))
    copies = []
    for tile in range(steps):
        value = partial[tile]
        for (high, low), at in zip(halves, places):
            value = value + dot3(high, low, cosines[tile, at], cosines[steps + tile, at], ((1,), (0,)))
        acc[tile] = value
        for layer in range(count):
            copies.append(
                pltpu.make_async_copy(
                    acc.at[tile, pl.ds(layer * rows, rows)],
                    out.at[table[slot + layer] - first, :, pl.ds(tile * step, step)],
                    sems.at[tile, layer],
                )
            )
            copies[-1].start()
    for copy in copies:
        copy.wait()


def along_y_rest(tiles, spacing, anchor, partial, pieces, slot, depth, before, parts):
    count, rows, _ = pieces[0].shape
    _, length, step = tiles.shape
    steps = length // step
    chained = before is not None
    return pl.pallas_call(
        functools.partial(y_rest_kernel, parts, slot, chained),
        out_shape=jax.ShapeDtypeStruct((depth, rows, length), jnp.float32),
        in_specs=[SMEM, SMEM] + [VMEM] * (2 + len(pieces)) + ([HBM] if chained else []),
        out_specs=HBM,
        scratch_shapes=[
            pltpu.VMEM((steps, count * rows, step), jnp.float32),
            pltpu.SMEM((depth,), jnp.int32),
            pltpu.SemaphoreType.DMA((steps, count)),
        ],
        input_output_aliases={4 + len(pieces): 0} if chained else {},
        compiler_params=params(length),
        cost_estimate=cost(2.0),
        name="along_y_rest",
    )(spacing, anchor, in_vmem(tiles), partial, *pieces, *([before] if chained else []))


def y_kernel(slot, chained, apart, spacing, anchor, cosines, *rest):
    out, token, a_high, a_low, acc, near, table, sems, more = rest[-9:]
    _, length, step = cosines.shape
    steps = length // step
    parts = length // LANES
    pieces = rest[: parts if apart else 1]
    token[...] = jnp.zeros(token.shape, jnp.float32)
    count, rows, _ = pieces[0].shape[-3:]
    depth = out.shape[0]
    if not apart:
        arrivals = [pltpu.make_async_copy(pieces[0].at[n], near.at[n], more.at[n]) for n in range(parts)]
        for arrival in arrivals:
            arrival.start()
    first = lax.axis_index("gx") * depth
    order_layers(table, 0, first, depth, spacing[0], anchor[0])
    row = lax.axis_index("gy")
    for part in range(parts):
        if apart:
            piece = pieces[part]
            cols = pl.ds(pl.multiple_of((row ^ partner(part, parts)) * LANES, LANES), LANES)
        else:
            arrivals[part].wait()
            piece = near.at[part]
            cols = pl.ds(part * LANES, LANES)
        for layer in range(count):
            high, low = split(piece[layer])
            at = pl.ds(layer * rows, rows)
            a_high[at, cols] = high
            a_low[at, cols] = low

    copies = []
    for tile in range(steps):
        acc[tile] = dot3(a_high[...], a_low[...], cosines[tile], cosines[steps + tile], ((1,), (0,)))
        for layer in range(count):
            copies.append(
                pltpu.make_async_copy(
                    acc.at[tile, pl.ds(layer * rows, rows)],
                    out.at[table[slot + layer] - first, :, pl.ds(tile * step, step)],
                    sems.at[tile, layer],
                )
            )
            copies[-1].start()
    for copy in copies:
        copy.wait()


def along_y(tiles, spacing, anchor, pieces, slot, depth, before, parts, after):
    apart = len(pieces) > 1
    count, rows, _ = pieces[0].shape[-3:]
    length = parts * LANES
    step = min(256, length)
    steps = length // step
    chained = before is not None
    near = (1, 8, LANES) if apart else pieces[0].shape[1:]
    pieces = pieces if apart else [in_hbm(pieces[0])]
    return pl.pallas_call(
        functools.partial(y_kernel, slot, chained, apart),
        out_shape=[jax.ShapeDtypeStruct((depth, rows, length), jnp.float32), TOKEN],
        in_specs=[SMEM, SMEM, VMEM]
        + [VMEM if apart else HBM] * len(pieces)
        + ([HBM] if chained else [])
        + [ANY] * len(after),
        out_specs=[HBM, VMEM],
        scratch_shapes=[
            pltpu.VMEM((count * rows, length), jnp.bfloat16),
            pltpu.VMEM((count * rows, length), jnp.bfloat16),
            pltpu.VMEM((steps, count * rows, step), jnp.float32),
            pltpu.VMEM((1 if apart else parts,) + near, jnp.float32),
            pltpu.SMEM((depth,), jnp.int32),
            pltpu.SemaphoreType.DMA((steps, count)),
            pltpu.SemaphoreType.DMA((parts,)),
        ],
        input_output_aliases={3 + len(pieces): 0} if chained else {},
        compiler_params=params(length),
        cost_estimate=cost(1.0 * count),
        name="along_y",
    )(spacing, anchor, in_vmem(tiles), *pieces, *([before] if chained else []), *after)


def swap(value, axis, k):
    size = lax.axis_size(axis)
    return lax.ppermute(value, axis, [(i, i ^ k) for i in range(size)])


def exchange(pieces, axis):
    return [swap(piece, axis, k) for piece, k in zip(pieces, partners(len(pieces) + 1))]


def swap_neighbours(first, second, axis):
    size = lax.axis_size(axis)
    answers = []
    for value, start in ((first, 0), (second, 1)):
        pairs = [(i, i + 1) for i in range(start, size - 1, 2)]
        answers.append(lax.ppermute(value, axis, pairs + [(j, i) for i, j in pairs]))
    return answers


def per_device(intensity, weight, spacing, anchor, reach):
    layers, rows, _ = intensity.shape
    groups = lax.axis_size("gx")
    parts = lax.axis_size("gy")
    depth = layers // groups
    held = hole_slots(depth)
    full = (rows * groups, LANES * parts)

    clean = depth - held
    early = min(EARLY, clean)
    late = clean - early

    def to_rows(spectrum, apart):
        if apart:
            return spectrum[:1] + exchange(spectrum[1:], "gy")
        return [lax.all_to_all(spectrum[0], "gy", split_axis=0, concat_axis=0, tiled=True)]

    chunks = []
    if early:
        gathered = gather_clean(spacing, anchor, intensity, groups, 0, early)
        first_pieces = exchange(gathered, "gx")
    v, w, own, one, other, *mine, token = punch(
        spacing, anchor, reach, intensity, weight, groups, held, early, late
    )
    sides = swap_neighbours(one, other, "gy")
    ends = swap_neighbours(*edges(v, w, own, *sides, []), "gx")
    if early:
        first_pieces = mine[:1] + first_pieces
        mine = mine[1:]
        *spectrum, token = along_x(first_pieces, parts, FIRST_APART, sides)
        chunks.append((0, to_rows(spectrum, FIRST_APART)))
    *filled, token = fill(
        spacing, anchor, reach, v, w, [own] + sides, ends, mine, groups, held, depth, full, [token]
    )
    tiles = jnp.asarray(np.concatenate(column_tiles(full[1], min(256, full[1]))))
    pieces = filled[:1] + exchange([filled[k] for k in partners(groups)], "gx")
    *spectrum, token = along_x(pieces, parts, LAST_APART, [token])
    chunks.append((early, to_rows(spectrum, LAST_APART)))
    out = None
    for slot, pieces in chunks[:-1]:
        out, token = along_y(tiles, spacing, anchor, pieces, slot, depth, out, parts, [token])
    slot, pieces = chunks[-1]
    some = early_pieces(parts)
    partial = along_y_part(tiles, pieces[:some], parts, [token])
    out = along_y_rest(tiles, spacing, anchor, partial, pieces[some:], slot, depth, out, parts)
    return out


def solution(mesh):
    in_specs = (P(None, "gx", "gy"), P(None, "gx", "gy"), P(), P(), P())
    out_specs = P("gx", "gy", None)
    return jax.shard_map(per_device, mesh=mesh, in_specs=in_specs, out_specs=out_specs, check_vma=False)
```

```python
import functools
import math

import jax
import jax.numpy as jnp
import numpy as np
from jax import lax
from jax.experimental import pallas as pl
from jax.experimental.pallas import tpu as pltpu
from jax.sharding import PartitionSpec as P

MIN_SPACING = 10
HALO = 3
LANES = 128
PACK = LANES // (2 * HALO)
FIRST_APART = False
LAST_APART = True
EARLY = 5
HBM = pl.BlockSpec(memory_space=pltpu.HBM)
ANY = pl.BlockSpec(memory_space=pl.ANY)
SMEM = pl.BlockSpec(memory_space=pltpu.SMEM)
VMEM = pl.BlockSpec(memory_space=pltpu.VMEM)


def hole_slots(depth):
    whole, left = divmod(depth, MIN_SPACING)
    return min(depth, 3 * whole + min(3, left))


@functools.lru_cache(maxsize=None)
def cosine_split(length):
    freq = np.arange(length, dtype=np.int64)
    phase = (freq[:, None] * (2 * freq[None, :] + 1)) % (4 * length)
    matrix = np.cos(phase * (math.pi / (2 * length))) * math.sqrt(2.0 / length)
    high = matrix.astype(jnp.bfloat16)
    low = (matrix - high.astype(np.float64)).astype(jnp.bfloat16)
    return high, low


def split(value):
    high = value.astype(jnp.bfloat16)
    return high, (value - high.astype(jnp.float32)).astype(jnp.bfloat16)


def params(length=0):
    return pltpu.CompilerParams(vmem_limit_bytes=8 * 2**20 + 6 * length * length)


def cost(micros):
    return pl.CostEstimate(flops=0, bytes_accessed=int(micros * 3.6e6), transcendentals=0)


TOKEN = jax.ShapeDtypeStruct((8, LANES), jnp.float32)


def partner(n, size):
    if n < 3 or size <= 4:
        return n
    if n < 5:
        return size - 1 if n == 3 else 3
    return size + 3 - n


def column_of(lane):
    turn = jnp.floor((lane.astype(jnp.float32) + 0.5) * (0.5 / HALO))
    return lane - 2 * HALO * turn.astype(jnp.int32)


def is_even(axis, shape):
    return jnp.full(shape, lax.rem(lax.axis_index(axis), 2)) == 0


def early_pieces(parts):
    return parts // 2 + 1


def partners(size):
    return [partner(n, size) for n in range(1, size)]


def in_hbm(value):
    return pltpu.with_memory_space_constraint(value, pltpu.HBM)


def in_vmem(value):
    return pltpu.with_memory_space_constraint(value, pltpu.VMEM)


def floor_mod(value, by):
    rest = lax.rem(value, by)
    return jnp.where(rest < 0, rest + by, rest)


def order_layers(table, at, first, depth, spacing, anchor):
    phase = floor_mod(first - anchor, spacing)
    front = jnp.int32(0)
    back = jnp.int32(depth - 1)
    for step in range(depth):
        hole = (phase <= 1) | (phase == spacing - 1)
        table[at + jnp.where(hole, back, front)] = first + step
        front = jnp.where(hole, front, front + 1)
        back = jnp.where(hole, back - 1, back)
        phase = jnp.where(phase + 1 == spacing, 0, phase + 1)


def is_hole_layer(layer, spacing, anchor):
    phase = floor_mod(layer - anchor, spacing)
    return (phase <= 1) | (phase == spacing - 1)


def squared_dist(position, spacing, anchor):
    step = spacing.astype(jnp.float32)
    from_anchor = (position - anchor).astype(jnp.float32)
    turns = jnp.floor((from_anchor + 0.5) / step)
    offset = from_anchor - turns * step
    dist = jnp.minimum(offset, step - offset)
    return dist * dist


def clean_copies(depth, some, slot, count, table, layers, outs, sems):
    me = lax.axis_index("gx")
    copies = []
    for n, k in enumerate(some):
        for part in range(count):
            layer = table[(me ^ k) * depth + slot + part]
            copies.append(
                pltpu.make_async_copy(layers.at[layer], outs[n].at[part], sems.at[n * count + part])
            )
    return copies


def gather_kernel(sizes, slot, count, spacing_in, anchor_in, layers, *rest):
    groups, depth = sizes
    outs, (spacing, anchor, table, sems, small) = rest[:-5], rest[-5:]
    first = pltpu.make_async_copy(spacing_in, spacing, small.at[0])
    second = pltpu.make_async_copy(anchor_in, anchor, small.at[1])
    first.start()
    second.start()
    first.wait()
    second.wait()
    for group in range(groups):
        order_layers(table, group * depth, group * depth, depth, spacing[0], anchor[0])
    copies = clean_copies(depth, partners(groups), slot, count, table, layers, outs, sems)
    for copy in copies:
        copy.start()
    for copy in copies:
        copy.wait()


def gather_clean(spacing, anchor, layers, groups, slot, count):
    depth = layers.shape[0] // groups
    return pl.pallas_call(
        functools.partial(gather_kernel, (groups, depth), slot, count),
        out_shape=[jax.ShapeDtypeStruct((count,) + layers.shape[1:], jnp.float32)] * (groups - 1),
        in_specs=[HBM] * 3,
        out_specs=[VMEM] * (groups - 1),
        scratch_shapes=[
            pltpu.SMEM(spacing.shape, jnp.int32),
            pltpu.SMEM(anchor.shape, jnp.int32),
            pltpu.SMEM((groups * depth,), jnp.int32),
            pltpu.SemaphoreType.DMA((groups * count,)),
            pltpu.SemaphoreType.DMA((2,)),
        ],
        compiler_params=params(),
        cost_estimate=cost(1.5),
        name="gather_clean",
    )(in_hbm(spacing), in_hbm(anchor), in_hbm(layers))


def punch_kernel(sizes, early, late, spacing, anchor, reach, layers, weights, v_out, w_out, sides_out, one_out, other_out, *rest):
    groups, depth, held = sizes
    outs, (token, table, sems, more, own_sems) = rest[:-5], rest[-5:]
    token[...] = jnp.zeros(token.shape, jnp.float32)
    rows = v_out.shape[1]
    total = groups * held
    x_start = lax.axis_index("gx") * rows
    y_start = lax.axis_index("gy") * LANES
    for group in range(groups):
        order_layers(table, group * depth, group * depth, depth, spacing[0], anchor[0])
    copies = []
    for at in range(total):
        layer = table[(at // held) * depth + depth - held + at % held]
        copies.append(pltpu.make_async_copy(layers.at[layer], v_out.at[at], sems.at[at]))
        copies.append(pltpu.make_async_copy(weights.at[layer], w_out.at[at], sems.at[total + at]))
    for copy in copies:
        copy.start()
    others = []
    if early:
        others += clean_copies(depth, [0], 0, early, table, layers, outs[:1], own_sems)
        outs = outs[1:]
    if late:
        others += clean_copies(depth, range(groups), early, late, table, layers, outs, more)
    for copy in others:
        copy.start()
    shape = (rows, LANES)
    x_at = x_start + lax.broadcasted_iota(jnp.int32, shape, 0)
    lane = lax.broadcasted_iota(jnp.int32, shape, 1)
    plane = squared_dist(x_at, spacing[1], anchor[1]) + squared_dist(y_start + lane, spacing[2], anchor[2])
    flat = plane <= reach[0].astype(jnp.float32)
    for copy in copies:
        copy.wait()
    for at in range(total):
        layer = table[(at // held) * depth + depth - held + at % held]
        tall = jnp.where(is_hole_layer(layer, spacing[0], anchor[0]), 1.0, 0.0)
        v_out[at] = jnp.where(flat & (jnp.full(shape, tall) > 0.5), 0.0, v_out[at])
    for pack in range(sides_out.shape[1]):
        for kind, ref in enumerate((v_out, w_out)):
            tile = jnp.zeros(shape, jnp.float32)
            for at in range(pack * PACK, min(total, (pack + 1) * PACK)):
                place = 2 * HALO * (at % PACK)
                here = (lane >= place) & (lane < place + 2 * HALO)
                tile = jnp.where(here, pltpu.roll(ref[at], place + HALO, 1), tile)
            sides_out[kind, pack] = tile
        inner = column_of(lane) < HALO
        value, weight = sides_out[0, pack], sides_out[1, pack]
        to_right = jnp.where(inner, value, pltpu.roll(weight, HALO, 1))
        to_left = jnp.where(inner, pltpu.roll(weight, LANES - HALO, 1), value)
        even = is_even("gy", shape)
        one_out[pack] = jnp.where(even, to_right, to_left)
        other_out[pack] = jnp.where(even, to_left, to_right)
    for copy in others:
        copy.wait()


def punch(spacing, anchor, reach, layers, weights, groups, held, early, late):
    depth = layers.shape[0] // groups
    total = groups * held
    packs = -(-total // PACK)
    tile = layers.shape[1:]
    clean = ([(early,)] if early else []) + ([(late,)] * groups if late else [])
    return pl.pallas_call(
        functools.partial(punch_kernel, (groups, depth, held), early, late),
        out_shape=[
            pltpu.VMEM(size + tile, jnp.float32)
            for size in [(total,), (total,), (2, packs), (packs,), (packs,)] + clean
        ]
        + [TOKEN],
        in_specs=[SMEM, SMEM, SMEM, HBM, HBM],
        out_specs=[VMEM] * (6 + len(clean)),
        scratch_shapes=[
            pltpu.SMEM((groups * depth,), jnp.int32),
            pltpu.SemaphoreType.DMA((2 * total,)),
            pltpu.SemaphoreType.DMA((groups * max(1, late),)),
            pltpu.SemaphoreType.DMA((max(1, early),)),
        ],
        compiler_params=params(),
        cost_estimate=cost(3.5),
        name="punch",
    )(spacing, anchor, reach, in_hbm(layers), in_hbm(weights))


def edge_kernel(v, w, own, one, other, *rest):
    outs = rest[-2:]
    rows = v.shape[1]
    even = lax.rem(lax.axis_index("gx"), 2)
    for parity in range(2):

        @pl.when(even == parity)
        def _():
            bottom, top = outs if parity == 0 else outs[::-1]
            at = 0
            for ref in (v, w, own, one, other):
                for array in [ref] if len(ref.shape) == 3 else [ref.at[0], ref.at[1]]:
                    count = array.shape[0]
                    top[at : at + count] = array[:, :8]
                    bottom[at : at + count] = array[:, rows - 8 :]
                    at += count


def edges(v, w, own, one, other, after):
    count = 2 * v.shape[0] + 4 * own.shape[1]
    return pl.pallas_call(
        edge_kernel,
        out_shape=[jax.ShapeDtypeStruct((count, 8, LANES), jnp.float32)] * 2,
        in_specs=[VMEM] * 5 + [ANY] * len(after),
        out_specs=[VMEM] * 2,
        compiler_params=params(),
        cost_estimate=cost(0.3),
        name="edges",
    )(in_vmem(v), in_vmem(w), own, one, other, *after)


def fill_kernel(sizes, spacing, anchor, reach, v_in, w_in, own, one_side, other_side, one_end, other_end, *rest):
    groups, depth, held, late, full_x, full_y = sizes
    outs, (token, table, result, beside) = rest[-groups - 4 : -4], rest[-4:]
    more = rest[:groups]
    token[...] = jnp.zeros(token.shape, jnp.float32)
    total = groups * held
    packs = own.shape[1]
    rows = v_in.shape[1]
    me = lax.axis_index("gx")
    x_start = me * rows
    y_start = lax.axis_index("gy") * LANES
    for group in range(groups):
        order_layers(table, group * depth, group * depth, depth, spacing[0], anchor[0])
    tall = rows + 16
    shape = (tall, LANES)
    lane = lax.broadcasted_iota(jnp.int32, shape, 1)
    x_at = x_start - 8 + lax.broadcasted_iota(jnp.int32, shape, 0)
    x_dist = squared_dist(x_at, spacing[1], anchor[1])
    x_inside = (x_at >= 0) & (x_at < full_x)
    column = column_of(lane)

    def holes_at(y_at):
        plane = x_dist + squared_dist(y_at, spacing[2], anchor[2])
        return (plane <= reach[0].astype(jnp.float32)) & x_inside & (y_at >= 0) & (y_at < full_y)

    even_x = is_even("gx", (8, LANES))
    even_y = is_even("gy", shape)

    def extended(ref, at, array):
        one, other = one_end[array], other_end[array]
        above = jnp.where(even_x, other, one)
        below = jnp.where(even_x, one, other)
        return jnp.concatenate([above, ref[at], below], axis=0)

    def down_rows(value):
        return pltpu.roll(value, 1, 0) + (value + value) + pltpu.roll(value, tall - 1, 0)

    def lanes(value, by):
        return pltpu.roll(value, by % LANES, 1)

    def inverse_of(hole, total_weight):
        return 1.0 / jnp.where(hole, total_weight, 1.0)

    def across(value):
        return lanes(value, 1) + (value + value) + lanes(value, -1)

    inner = column < HALO
    for pack in range(packs):
        at_end = 2 * total + pack
        mine = [extended(own, (kind, pack), at_end + kind * packs) for kind in range(2)]
        one_from = extended(one_side, pack, at_end + 2 * packs)
        other_from = extended(other_side, pack, at_end + 3 * packs)
        left = jnp.where(even_y, other_from, one_from)
        right = jnp.where(even_y, one_from, other_from)
        left, right = (left, lanes(left, -HALO)), (right, lanes(right, HALO))
        found = []
        for low, high, start in ((left, mine, -HALO), (mine, right, LANES - HALO)):
            tiles = [jnp.where(inner, one, other) for one, other in zip(low, high)]
            value, weight = tiles
            hole = holes_at(y_start + start + column)
            sums = down_rows(weight)
            kept = [sums]
            inverse = inverse_of(hole, across(sums))
            for sweep in range(3):
                sums = down_rows(weight * value)
                kept.append(sums)
                if sweep < 2:
                    value = jnp.where(hole, across(sums) * inverse, value)
            found.append(kept)
        for n in range(4):
            beside[pack, n] = jnp.where(column == HALO - 2, lanes(found[1][n], -2), found[0][n])

    flat = holes_at(y_start + lane)
    flat_f = jnp.where(flat, 1.0, 0.0)

    def one(index, carry):
        group = me ^ index
        values, weights, holes, edges_at = [], [], [], []
        for slot in range(held):
            at = group * held + slot
            layer = table[group * depth + depth - held + slot]
            swept = jnp.where(is_hole_layer(layer, spacing[0], anchor[0]), 1.0, 0.0)
            values.append(extended(v_in, at, at))
            weights.append(extended(w_in, at, total + at))
            holes.append(flat_f * swept > 0.5)
            to_edge = 2 * LANES - (2 * HALO * lax.rem(at, PACK) + HALO - 1)
            edges_at.append((lax.div(at, PACK), jnp.where(to_edge >= LANES, to_edge - LANES, to_edge)))

        def smooth(arrays, n):
            arrays = [down_rows(array) for array in arrays]
            edges = [pltpu.roll(beside[pack, n], to_edge, 1) for pack, to_edge in edges_at]
            before = [jnp.where(lane == 0, edge, lanes(array, 1)) for edge, array in zip(edges, arrays)]
            after = [jnp.where(lane == LANES - 1, edge, lanes(array, -1)) for edge, array in zip(edges, arrays)]
            return [low + (array + array) + high for low, array, high in zip(before, arrays, after)]

        inverses = [inverse_of(hole, value) for hole, value in zip(holes, smooth(weights, 0))]
        for sweep in range(3):
            sums = smooth([weight * value for weight, value in zip(weights, values)], sweep + 1)
            values = [
                jnp.where(hole, value * inverse, old)
                for hole, value, inverse, old in zip(holes, sums, inverses, values)
            ]
        for slot in range(held):
            result[index * held + slot] = values[slot][8 : 8 + rows]
        return carry

    lax.fori_loop(0, groups, one, 0)
    for n in range(groups):
        if late:
            outs[n][:late] = more[n][...]
        outs[n][late:] = result[n * held : (n + 1) * held]


def fill(spacing, anchor, reach, v, w, sides, ends, late, groups, held, depth, full, after):
    count = late[0].shape[0] if late else 0
    rows = v.shape[1]
    return pl.pallas_call(
        functools.partial(fill_kernel, (groups, depth, held, count) + full),
        out_shape=[jax.ShapeDtypeStruct((count + held, rows, LANES), jnp.float32)] * groups + [TOKEN],
        in_specs=[SMEM] * 3 + [VMEM] * (7 + len(late)) + [ANY] * len(after),
        out_specs=[VMEM] * (groups + 1),
        scratch_shapes=[
            pltpu.SMEM((groups * depth,), jnp.int32),
            pltpu.VMEM((groups * held, rows, LANES), jnp.float32),
            pltpu.VMEM((sides[0].shape[1], 4, rows + 16, LANES), jnp.float32),
        ],
        compiler_params=params(),
        cost_estimate=cost(7.0),
        name="fill",
    )(spacing, anchor, reach, in_vmem(v), in_vmem(w), *sides, *ends, *late, *after)


def dot3(a_high, a_low, b_high, b_low, dims):
    def dot(a, b):
        return lax.dot_general(a, b, (dims, ((), ())), preferred_element_type=jnp.float32)

    return dot(a_high, b_high) + (dot(a_high, b_low) + dot(a_low, b_high))


def x_kernel(groups, made, step, c_high, c_low, *rest):
    pieces = rest[:groups]
    outs, (token, b_high, b_low, acc, sems) = rest[-5 - made : -5], rest[-5:]
    token[...] = jnp.zeros(token.shape, jnp.float32)
    apart = len(outs) > 1
    count, rows, _ = pieces[0].shape
    out_rows = outs[0].shape[-2]
    length = c_high.shape[0]
    parts = length // out_rows
    me = lax.axis_index("gx")
    for k in range(groups):
        at = pl.ds(pl.multiple_of((me ^ partner(k, groups)) * rows, rows), rows)
        for layer in range(count):
            high, low = split(pieces[k][layer])
            cols = pl.ds(layer * LANES, LANES)
            b_high[at, cols] = high
            b_low[at, cols] = low
    each = step // out_rows
    copies = []
    for tile in range(length // step):
        at = pl.ds(tile * step, step)
        value = dot3(c_high[at], c_low[at], b_high[...], b_low[...], ((1,), (0,)))
        if apart:
            acc[at] = value
            continue
        for part in range(each):
            for layer in range(count):
                acc[tile * each + part, layer] = value[
                    part * out_rows : (part + 1) * out_rows, layer * LANES : (layer + 1) * LANES
                ]
        some = pl.ds(tile * each, each)
        copies.append(pltpu.make_async_copy(acc.at[some], outs[0].at[some], sems.at[tile]))
        copies[-1].start()
    for copy in copies:
        copy.wait()
    if apart:
        row = lax.axis_index("gy")
        for k in range(parts):
            at = pl.ds(pl.multiple_of((row ^ partner(k, parts)) * out_rows, out_rows), out_rows)
            for layer in range(count):
                outs[k][layer] = acc[at, pl.ds(layer * LANES, LANES)]


def along_x(pieces, parts, apart, after):
    groups = len(pieces)
    count, rows, _ = pieces[0].shape
    length = rows * groups
    step = min(512 if apart else 256, length)
    high, low = cosine_split(length)
    tile = (count, length // parts, LANES)
    if apart:
        shapes = [jax.ShapeDtypeStruct(tile, jnp.float32)] * parts
    else:
        shapes = [pltpu.HBM((parts,) + tile, jnp.float32)]
    return pl.pallas_call(
        functools.partial(x_kernel, groups, len(shapes), step),
        out_shape=shapes + [TOKEN],
        in_specs=[VMEM] * (2 + groups) + [ANY] * len(after),
        out_specs=[VMEM if apart else HBM] * len(shapes) + [VMEM],
        scratch_shapes=[
            pltpu.VMEM((length, count * LANES), jnp.bfloat16),
            pltpu.VMEM((length, count * LANES), jnp.bfloat16),
            pltpu.VMEM((length, count * LANES) if apart else (parts,) + tile, jnp.float32),
            pltpu.SemaphoreType.DMA((length // step,)),
        ],
        compiler_params=params(length),
        cost_estimate=cost(0.4 * count),
        name="along_x",
    )(high, low, *pieces, *after)


def column_tiles(length, step):
    return [part.T.reshape(length, -1, step).swapaxes(0, 1) for part in cosine_split(length)]


def y_part_kernel(parts, cosines, *rest):
    out, a_high, a_low = rest[-3:]
    steps = out.shape[0]
    early = early_pieces(parts)
    pieces = rest[:early]
    count, rows, _ = pieces[0].shape
    row = lax.axis_index("gy")
    for n in range(parts):
        cols = pl.ds(pl.multiple_of((row ^ partner(n, parts)) * LANES, LANES), LANES)
        for layer in range(count):
            at = pl.ds(layer * rows, rows)
            if n < early:
                a_high[at, cols], a_low[at, cols] = split(pieces[n][layer])
            else:
                a_high[at, cols] = jnp.zeros((rows, LANES), jnp.bfloat16)
                a_low[at, cols] = jnp.zeros((rows, LANES), jnp.bfloat16)
    for tile in range(steps):
        out[tile] = dot3(a_high[...], a_low[...], cosines[tile], cosines[steps + tile], ((1,), (0,)))


def along_y_part(tiles, pieces, parts, after):
    count, rows, _ = pieces[0].shape
    _, length, step = tiles.shape
    return pl.pallas_call(
        functools.partial(y_part_kernel, parts),
        out_shape=jax.ShapeDtypeStruct((length // step, count * rows, step), jnp.float32),
        in_specs=[VMEM] * (1 + len(pieces)) + [ANY] * len(after),
        out_specs=VMEM,
        scratch_shapes=[pltpu.VMEM((count * rows, length), jnp.bfloat16)] * 2,
        compiler_params=params(length),
        cost_estimate=cost(2.0),
        name="along_y_part",
    )(in_vmem(tiles), *pieces, *after)


def y_rest_kernel(parts, slot, chained, spacing, anchor, cosines, partial, *rest):
    out, acc, table, sems = rest[-4:]
    early = early_pieces(parts)
    pieces = rest[: parts - early]
    steps = partial.shape[0]
    step = partial.shape[2]
    count, rows, _ = pieces[0].shape
    depth = out.shape[0]
    first = lax.axis_index("gx") * depth
    order_layers(table, 0, first, depth, spacing[0], anchor[0])
    row = lax.axis_index("gy")
    halves, places = [], []
    for n, piece in enumerate(pieces):
        halves.append(split(jnp.concatenate([piece[layer] for layer in range(count)], axis=0)))
        start = (row ^ partner(early + n, parts)) * LANES
        places.append(pl.ds(pl.multiple_of(start, LANES), LANES))
    copies = []
    for tile in range(steps):
        value = partial[tile]
        for (high, low), at in zip(halves, places):
            value = value + dot3(high, low, cosines[tile, at], cosines[steps + tile, at], ((1,), (0,)))
        acc[tile] = value
        for layer in range(count):
            copies.append(
                pltpu.make_async_copy(
                    acc.at[tile, pl.ds(layer * rows, rows)],
                    out.at[table[slot + layer] - first, :, pl.ds(tile * step, step)],
                    sems.at[tile, layer],
                )
            )
            copies[-1].start()
    for copy in copies:
        copy.wait()


def along_y_rest(tiles, spacing, anchor, partial, pieces, slot, depth, before, parts):
    count, rows, _ = pieces[0].shape
    _, length, step = tiles.shape
    steps = length // step
    chained = before is not None
    return pl.pallas_call(
        functools.partial(y_rest_kernel, parts, slot, chained),
        out_shape=jax.ShapeDtypeStruct((depth, rows, length), jnp.float32),
        in_specs=[SMEM, SMEM] + [VMEM] * (2 + len(pieces)) + ([HBM] if chained else []),
        out_specs=HBM,
        scratch_shapes=[
            pltpu.VMEM((steps, count * rows, step), jnp.float32),
            pltpu.SMEM((depth,), jnp.int32),
            pltpu.SemaphoreType.DMA((steps, count)),
        ],
        input_output_aliases={4 + len(pieces): 0} if chained else {},
        compiler_params=params(length),
        cost_estimate=cost(2.0),
        name="along_y_rest",
    )(spacing, anchor, in_vmem(tiles), partial, *pieces, *([before] if chained else []))


def y_kernel(slot, chained, apart, spacing, anchor, cosines, *rest):
    out, token, a_high, a_low, acc, near, table, sems, more = rest[-9:]
    _, length, step = cosines.shape
    steps = length // step
    parts = length // LANES
    pieces = rest[: parts if apart else 1]
    token[...] = jnp.zeros(token.shape, jnp.float32)
    count, rows, _ = pieces[0].shape[-3:]
    depth = out.shape[0]
    if not apart:
        arrivals = [pltpu.make_async_copy(pieces[0].at[n], near.at[n], more.at[n]) for n in range(parts)]
        for arrival in arrivals:
            arrival.start()
    first = lax.axis_index("gx") * depth
    order_layers(table, 0, first, depth, spacing[0], anchor[0])
    row = lax.axis_index("gy")
    for part in range(parts):
        if apart:
            piece = pieces[part]
            cols = pl.ds(pl.multiple_of((row ^ partner(part, parts)) * LANES, LANES), LANES)
        else:
            arrivals[part].wait()
            piece = near.at[part]
            cols = pl.ds(part * LANES, LANES)
        for layer in range(count):
            high, low = split(piece[layer])
            at = pl.ds(layer * rows, rows)
            a_high[at, cols] = high
            a_low[at, cols] = low

    copies = []
    for tile in range(steps):
        acc[tile] = dot3(a_high[...], a_low[...], cosines[tile], cosines[steps + tile], ((1,), (0,)))
        for layer in range(count):
            copies.append(
                pltpu.make_async_copy(
                    acc.at[tile, pl.ds(layer * rows, rows)],
                    out.at[table[slot + layer] - first, :, pl.ds(tile * step, step)],
                    sems.at[tile, layer],
                )
            )
            copies[-1].start()
    for copy in copies:
        copy.wait()


def along_y(tiles, spacing, anchor, pieces, slot, depth, before, parts, after):
    apart = len(pieces) > 1
    count, rows, _ = pieces[0].shape[-3:]
    length = parts * LANES
    step = min(256, length)
    steps = length // step
    chained = before is not None
    near = (1, 8, LANES) if apart else pieces[0].shape[1:]
    pieces = pieces if apart else [in_hbm(pieces[0])]
    return pl.pallas_call(
        functools.partial(y_kernel, slot, chained, apart),
        out_shape=[jax.ShapeDtypeStruct((depth, rows, length), jnp.float32), TOKEN],
        in_specs=[SMEM, SMEM, VMEM]
        + [VMEM if apart else HBM] * len(pieces)
        + ([HBM] if chained else [])
        + [ANY] * len(after),
        out_specs=[HBM, VMEM],
        scratch_shapes=[
            pltpu.VMEM((count * rows, length), jnp.bfloat16),
            pltpu.VMEM((count * rows, length), jnp.bfloat16),
            pltpu.VMEM((steps, count * rows, step), jnp.float32),
            pltpu.VMEM((1 if apart else parts,) + near, jnp.float32),
            pltpu.SMEM((depth,), jnp.int32),
            pltpu.SemaphoreType.DMA((steps, count)),
            pltpu.SemaphoreType.DMA((parts,)),
        ],
        input_output_aliases={3 + len(pieces): 0} if chained else {},
        compiler_params=params(length),
        cost_estimate=cost(1.0 * count),
        name="along_y",
    )(spacing, anchor, in_vmem(tiles), *pieces, *([before] if chained else []), *after)


def swap(value, axis, k):
    size = lax.axis_size(axis)
    return lax.ppermute(value, axis, [(i, i ^ k) for i in range(size)])


def exchange(pieces, axis):
    return [swap(piece, axis, k) for piece, k in zip(pieces, partners(len(pieces) + 1))]


def swap_neighbours(first, second, axis):
    size = lax.axis_size(axis)
    answers = []
    for value, start in ((first, 0), (second, 1)):
        pairs = [(i, i + 1) for i in range(start, size - 1, 2)]
        answers.append(lax.ppermute(value, axis, pairs + [(j, i) for i, j in pairs]))
    return answers


def per_device(intensity, weight, spacing, anchor, reach):
    layers, rows, _ = intensity.shape
    groups = lax.axis_size("gx")
    parts = lax.axis_size("gy")
    depth = layers // groups
    held = hole_slots(depth)
    full = (rows * groups, LANES * parts)

    clean = depth - held
    early = min(EARLY, clean)
    late = clean - early

    def to_rows(spectrum, apart):
        if apart:
            return spectrum[:1] + exchange(spectrum[1:], "gy")
        return [lax.all_to_all(spectrum[0], "gy", split_axis=0, concat_axis=0, tiled=True)]

    chunks = []
    if early:
        gathered = gather_clean(spacing, anchor, intensity, groups, 0, early)
        first_pieces = exchange(gathered, "gx")
    v, w, own, one, other, *mine, token = punch(
        spacing, anchor, reach, intensity, weight, groups, held, early, late
    )
    sides = swap_neighbours(one, other, "gy")
    ends = swap_neighbours(*edges(v, w, own, *sides, []), "gx")
    if early:
        first_pieces = mine[:1] + first_pieces
        mine = mine[1:]
        *spectrum, token = along_x(first_pieces, parts, FIRST_APART, sides)
        chunks.append((0, to_rows(spectrum, FIRST_APART)))
    *filled, token = fill(
        spacing, anchor, reach, v, w, [own] + sides, ends, mine, groups, held, depth, full, [token]
    )
    tiles = jnp.asarray(np.concatenate(column_tiles(full[1], min(256, full[1]))))
    pieces = filled[:1] + exchange([filled[k] for k in partners(groups)], "gx")
    *spectrum, token = along_x(pieces, parts, LAST_APART, [token])
    chunks.append((early, to_rows(spectrum, LAST_APART)))
    out = None
    for slot, pieces in chunks[:-1]:
        out, token = along_y(tiles, spacing, anchor, pieces, slot, depth, out, parts, [token])
    slot, pieces = chunks[-1]
    some = early_pieces(parts)
    partial = along_y_part(tiles, pieces[:some], parts, [token])
    out = along_y_rest(tiles, spacing, anchor, partial, pieces[some:], slot, depth, out, parts)
    return out


def solution(mesh):
    in_specs = (P(None, "gx", "gy"), P(None, "gx", "gy"), P(), P(), P())
    out_specs = P("gx", "gy", None)
    return jax.shard_map(per_device, mesh=mesh, in_specs=in_specs, out_specs=out_specs, check_vma=False)
```

```python
import functools
import math

import jax
import jax.numpy as jnp
import numpy as np
from jax import lax
from jax.experimental import pallas as pl
from jax.experimental.pallas import tpu as pltpu
from jax.sharding import PartitionSpec as P

MIN_SPACING = 10
HALO = 3
LANES = 128
PACK = LANES // (2 * HALO)
FIRST_APART = False
LAST_APART = True
EARLY = 5
HBM = pl.BlockSpec(memory_space=pltpu.HBM)
ANY = pl.BlockSpec(memory_space=pl.ANY)
SMEM = pl.BlockSpec(memory_space=pltpu.SMEM)
VMEM = pl.BlockSpec(memory_space=pltpu.VMEM)


def hole_slots(depth):
    whole, left = divmod(depth, MIN_SPACING)
    return min(depth, 3 * whole + min(3, left))


@functools.lru_cache(maxsize=None)
def cosine_split(length):
    freq = np.arange(length, dtype=np.int64)
    phase = (freq[:, None] * (2 * freq[None, :] + 1)) % (4 * length)
    matrix = np.cos(phase * (math.pi / (2 * length))) * math.sqrt(2.0 / length)
    high = matrix.astype(jnp.bfloat16)
    low = (matrix - high.astype(np.float64)).astype(jnp.bfloat16)
    return high, low


def split(value):
    high = value.astype(jnp.bfloat16)
    return high, (value - high.astype(jnp.float32)).astype(jnp.bfloat16)


def params(length=0):
    return pltpu.CompilerParams(vmem_limit_bytes=8 * 2**20 + 6 * length * length)


def cost(micros):
    return pl.CostEstimate(flops=0, bytes_accessed=int(micros * 3.6e6), transcendentals=0)


TOKEN = jax.ShapeDtypeStruct((8, LANES), jnp.float32)


def partner(n, size):
    if n < 3 or size <= 4:
        return n
    if n < 5:
        return size - 1 if n == 3 else 3
    return size + 3 - n


def column_of(lane):
    turn = jnp.floor((lane.astype(jnp.float32) + 0.5) * (0.5 / HALO))
    return lane - 2 * HALO * turn.astype(jnp.int32)


def is_even(axis, shape):
    return jnp.full(shape, lax.rem(lax.axis_index(axis), 2)) == 0


def early_pieces(parts):
    return parts // 2 + 2


def partners(size):
    return [partner(n, size) for n in range(1, size)]


def in_hbm(value):
    return pltpu.with_memory_space_constraint(value, pltpu.HBM)


def in_vmem(value):
    return pltpu.with_memory_space_constraint(value, pltpu.VMEM)


def floor_mod(value, by):
    rest = lax.rem(value, by)
    return jnp.where(rest < 0, rest + by, rest)


def order_layers(table, at, first, depth, spacing, anchor):
    phase = floor_mod(first - anchor, spacing)
    front = jnp.int32(0)
    back = jnp.int32(depth - 1)
    for step in range(depth):
        hole = (phase <= 1) | (phase == spacing - 1)
        table[at + jnp.where(hole, back, front)] = first + step
        front = jnp.where(hole, front, front + 1)
        back = jnp.where(hole, back - 1, back)
        phase = jnp.where(phase + 1 == spacing, 0, phase + 1)


def is_hole_layer(layer, spacing, anchor):
    phase = floor_mod(layer - anchor, spacing)
    return (phase <= 1) | (phase == spacing - 1)


def squared_dist(position, spacing, anchor):
    step = spacing.astype(jnp.float32)
    from_anchor = (position - anchor).astype(jnp.float32)
    turns = jnp.floor((from_anchor + 0.5) / step)
    offset = from_anchor - turns * step
    dist = jnp.minimum(offset, step - offset)
    return dist * dist


def clean_copies(depth, some, slot, count, table, layers, outs, sems):
    me = lax.axis_index("gx")
    copies = []
    for n, k in enumerate(some):
        for part in range(count):
            layer = table[(me ^ k) * depth + slot + part]
            copies.append(
                pltpu.make_async_copy(layers.at[layer], outs[n].at[part], sems.at[n * count + part])
            )
    return copies


def gather_kernel(sizes, slot, count, spacing_in, anchor_in, layers, *rest):
    groups, depth = sizes
    outs, (spacing, anchor, table, sems, small) = rest[:-5], rest[-5:]
    first = pltpu.make_async_copy(spacing_in, spacing, small.at[0])
    second = pltpu.make_async_copy(anchor_in, anchor, small.at[1])
    first.start()
    second.start()
    first.wait()
    second.wait()
    for group in range(groups):
        order_layers(table, group * depth, group * depth, depth, spacing[0], anchor[0])
    copies = clean_copies(depth, partners(groups), slot, count, table, layers, outs, sems)
    for copy in copies:
        copy.start()
    for copy in copies:
        copy.wait()


def gather_clean(spacing, anchor, layers, groups, slot, count):
    depth = layers.shape[0] // groups
    return pl.pallas_call(
        functools.partial(gather_kernel, (groups, depth), slot, count),
        out_shape=[jax.ShapeDtypeStruct((count,) + layers.shape[1:], jnp.float32)] * (groups - 1),
        in_specs=[HBM] * 3,
        out_specs=[VMEM] * (groups - 1),
        scratch_shapes=[
            pltpu.SMEM(spacing.shape, jnp.int32),
            pltpu.SMEM(anchor.shape, jnp.int32),
            pltpu.SMEM((groups * depth,), jnp.int32),
            pltpu.SemaphoreType.DMA((groups * count,)),
            pltpu.SemaphoreType.DMA((2,)),
        ],
        compiler_params=params(),
        cost_estimate=cost(1.5),
        name="gather_clean",
    )(in_hbm(spacing), in_hbm(anchor), in_hbm(layers))


def punch_kernel(sizes, early, late, spacing, anchor, reach, layers, weights, v_out, w_out, sides_out, one_out, other_out, *rest):
    groups, depth, held = sizes
    outs, (token, table, sems, more, own_sems) = rest[:-5], rest[-5:]
    token[...] = jnp.zeros(token.shape, jnp.float32)
    rows = v_out.shape[1]
    total = groups * held
    x_start = lax.axis_index("gx") * rows
    y_start = lax.axis_index("gy") * LANES
    for group in range(groups):
        order_layers(table, group * depth, group * depth, depth, spacing[0], anchor[0])
    copies = []
    for at in range(total):
        layer = table[(at // held) * depth + depth - held + at % held]
        copies.append(pltpu.make_async_copy(layers.at[layer], v_out.at[at], sems.at[at]))
        copies.append(pltpu.make_async_copy(weights.at[layer], w_out.at[at], sems.at[total + at]))
    for copy in copies:
        copy.start()
    others = []
    if early:
        others += clean_copies(depth, [0], 0, early, table, layers, outs[:1], own_sems)
        outs = outs[1:]
    if late:
        others += clean_copies(depth, range(groups), early, late, table, layers, outs, more)
    for copy in others:
        copy.start()
    shape = (rows, LANES)
    x_at = x_start + lax.broadcasted_iota(jnp.int32, shape, 0)
    lane = lax.broadcasted_iota(jnp.int32, shape, 1)
    plane = squared_dist(x_at, spacing[1], anchor[1]) + squared_dist(y_start + lane, spacing[2], anchor[2])
    flat = plane <= reach[0].astype(jnp.float32)
    for copy in copies:
        copy.wait()
    for at in range(total):
        layer = table[(at // held) * depth + depth - held + at % held]
        tall = jnp.where(is_hole_layer(layer, spacing[0], anchor[0]), 1.0, 0.0)
        v_out[at] = jnp.where(flat & (jnp.full(shape, tall) > 0.5), 0.0, v_out[at])
    for pack in range(sides_out.shape[1]):
        for kind, ref in enumerate((v_out, w_out)):
            tile = jnp.zeros(shape, jnp.float32)
            for at in range(pack * PACK, min(total, (pack + 1) * PACK)):
                place = 2 * HALO * (at % PACK)
                here = (lane >= place) & (lane < place + 2 * HALO)
                tile = jnp.where(here, pltpu.roll(ref[at], place + HALO, 1), tile)
            sides_out[kind, pack] = tile
        inner = column_of(lane) < HALO
        value, weight = sides_out[0, pack], sides_out[1, pack]
        to_right = jnp.where(inner, value, pltpu.roll(weight, HALO, 1))
        to_left = jnp.where(inner, pltpu.roll(weight, LANES - HALO, 1), value)
        even = is_even("gy", shape)
        one_out[pack] = jnp.where(even, to_right, to_left)
        other_out[pack] = jnp.where(even, to_left, to_right)
    for copy in others:
        copy.wait()


def punch(spacing, anchor, reach, layers, weights, groups, held, early, late):
    depth = layers.shape[0] // groups
    total = groups * held
    packs = -(-total // PACK)
    tile = layers.shape[1:]
    clean = ([(early,)] if early else []) + ([(late,)] * groups if late else [])
    return pl.pallas_call(
        functools.partial(punch_kernel, (groups, depth, held), early, late),
        out_shape=[
            pltpu.VMEM(size + tile, jnp.float32)
            for size in [(total,), (total,), (2, packs), (packs,), (packs,)] + clean
        ]
        + [TOKEN],
        in_specs=[SMEM, SMEM, SMEM, HBM, HBM],
        out_specs=[VMEM] * (6 + len(clean)),
        scratch_shapes=[
            pltpu.SMEM((groups * depth,), jnp.int32),
            pltpu.SemaphoreType.DMA((2 * total,)),
            pltpu.SemaphoreType.DMA((groups * max(1, late),)),
            pltpu.SemaphoreType.DMA((max(1, early),)),
        ],
        compiler_params=params(),
        cost_estimate=cost(3.5),
        name="punch",
    )(spacing, anchor, reach, in_hbm(layers), in_hbm(weights))


def edge_kernel(v, w, own, one, other, *rest):
    outs = rest[-2:]
    rows = v.shape[1]
    even = lax.rem(lax.axis_index("gx"), 2)
    for parity in range(2):

        @pl.when(even == parity)
        def _():
            bottom, top = outs if parity == 0 else outs[::-1]
            at = 0
            for ref in (v, w, own, one, other):
                for array in [ref] if len(ref.shape) == 3 else [ref.at[0], ref.at[1]]:
                    count = array.shape[0]
                    top[at : at + count] = array[:, :8]
                    bottom[at : at + count] = array[:, rows - 8 :]
                    at += count


def edges(v, w, own, one, other, after):
    count = 2 * v.shape[0] + 4 * own.shape[1]
    return pl.pallas_call(
        edge_kernel,
        out_shape=[jax.ShapeDtypeStruct((count, 8, LANES), jnp.float32)] * 2,
        in_specs=[VMEM] * 5 + [ANY] * len(after),
        out_specs=[VMEM] * 2,
        compiler_params=params(),
        cost_estimate=cost(0.3),
        name="edges",
    )(in_vmem(v), in_vmem(w), own, one, other, *after)


def fill_kernel(sizes, spacing, anchor, reach, v_in, w_in, own, one_side, other_side, one_end, other_end, *rest):
    groups, depth, held, late, full_x, full_y = sizes
    outs, (token, table, result, beside) = rest[-groups - 4 : -4], rest[-4:]
    more = rest[:groups]
    token[...] = jnp.zeros(token.shape, jnp.float32)
    total = groups * held
    packs = own.shape[1]
    rows = v_in.shape[1]
    me = lax.axis_index("gx")
    x_start = me * rows
    y_start = lax.axis_index("gy") * LANES
    for group in range(groups):
        order_layers(table, group * depth, group * depth, depth, spacing[0], anchor[0])
    tall = rows + 16
    shape = (tall, LANES)
    lane = lax.broadcasted_iota(jnp.int32, shape, 1)
    x_at = x_start - 8 + lax.broadcasted_iota(jnp.int32, shape, 0)
    x_dist = squared_dist(x_at, spacing[1], anchor[1])
    x_inside = (x_at >= 0) & (x_at < full_x)
    column = column_of(lane)

    def holes_at(y_at):
        plane = x_dist + squared_dist(y_at, spacing[2], anchor[2])
        return (plane <= reach[0].astype(jnp.float32)) & x_inside & (y_at >= 0) & (y_at < full_y)

    even_x = is_even("gx", (8, LANES))
    even_y = is_even("gy", shape)

    def extended(ref, at, array):
        one, other = one_end[array], other_end[array]
        above = jnp.where(even_x, other, one)
        below = jnp.where(even_x, one, other)
        return jnp.concatenate([above, ref[at], below], axis=0)

    def down_rows(value):
        return pltpu.roll(value, 1, 0) + (value + value) + pltpu.roll(value, tall - 1, 0)

    def lanes(value, by):
        return pltpu.roll(value, by % LANES, 1)

    def inverse_of(hole, total_weight):
        return 1.0 / jnp.where(hole, total_weight, 1.0)

    def across(value):
        return lanes(value, 1) + (value + value) + lanes(value, -1)

    inner = column < HALO
    for pack in range(packs):
        at_end = 2 * total + pack
        mine = [extended(own, (kind, pack), at_end + kind * packs) for kind in range(2)]
        one_from = extended(one_side, pack, at_end + 2 * packs)
        other_from = extended(other_side, pack, at_end + 3 * packs)
        left = jnp.where(even_y, other_from, one_from)
        right = jnp.where(even_y, one_from, other_from)
        left, right = (left, lanes(left, -HALO)), (right, lanes(right, HALO))
        found = []
        for low, high, start in ((left, mine, -HALO), (mine, right, LANES - HALO)):
            tiles = [jnp.where(inner, one, other) for one, other in zip(low, high)]
            value, weight = tiles
            hole = holes_at(y_start + start + column)
            sums = down_rows(weight)
            kept = [sums]
            inverse = inverse_of(hole, across(sums))
            for sweep in range(3):
                sums = down_rows(weight * value)
                kept.append(sums)
                if sweep < 2:
                    value = jnp.where(hole, across(sums) * inverse, value)
            found.append(kept)
        for n in range(4):
            beside[pack, n] = jnp.where(column == HALO - 2, lanes(found[1][n], -2), found[0][n])

    flat = holes_at(y_start + lane)
    flat_f = jnp.where(flat, 1.0, 0.0)

    def one(index, carry):
        group = me ^ index
        values, weights, holes, edges_at = [], [], [], []
        for slot in range(held):
            at = group * held + slot
            layer = table[group * depth + depth - held + slot]
            swept = jnp.where(is_hole_layer(layer, spacing[0], anchor[0]), 1.0, 0.0)
            values.append(extended(v_in, at, at))
            weights.append(extended(w_in, at, total + at))
            holes.append(flat_f * swept > 0.5)
            to_edge = 2 * LANES - (2 * HALO * lax.rem(at, PACK) + HALO - 1)
            edges_at.append((lax.div(at, PACK), jnp.where(to_edge >= LANES, to_edge - LANES, to_edge)))

        def smooth(arrays, n):
            arrays = [down_rows(array) for array in arrays]
            edges = [pltpu.roll(beside[pack, n], to_edge, 1) for pack, to_edge in edges_at]
            before = [jnp.where(lane == 0, edge, lanes(array, 1)) for edge, array in zip(edges, arrays)]
            after = [jnp.where(lane == LANES - 1, edge, lanes(array, -1)) for edge, array in zip(edges, arrays)]
            return [low + (array + array) + high for low, array, high in zip(before, arrays, after)]

        inverses = [inverse_of(hole, value) for hole, value in zip(holes, smooth(weights, 0))]
        for sweep in range(3):
            sums = smooth([weight * value for weight, value in zip(weights, values)], sweep + 1)
            values = [
                jnp.where(hole, value * inverse, old)
                for hole, value, inverse, old in zip(holes, sums, inverses, values)
            ]
        for slot in range(held):
            result[index * held + slot] = values[slot][8 : 8 + rows]
        return carry

    lax.fori_loop(0, groups, one, 0)
    for n in range(groups):
        if late:
            outs[n][:late] = more[n][...]
        outs[n][late:] = result[n * held : (n + 1) * held]


def fill(spacing, anchor, reach, v, w, sides, ends, late, groups, held, depth, full, after):
    count = late[0].shape[0] if late else 0
    rows = v.shape[1]
    return pl.pallas_call(
        functools.partial(fill_kernel, (groups, depth, held, count) + full),
        out_shape=[jax.ShapeDtypeStruct((count + held, rows, LANES), jnp.float32)] * groups + [TOKEN],
        in_specs=[SMEM] * 3 + [VMEM] * (7 + len(late)) + [ANY] * len(after),
        out_specs=[VMEM] * (groups + 1),
        scratch_shapes=[
            pltpu.SMEM((groups * depth,), jnp.int32),
            pltpu.VMEM((groups * held, rows, LANES), jnp.float32),
            pltpu.VMEM((sides[0].shape[1], 4, rows + 16, LANES), jnp.float32),
        ],
        compiler_params=params(),
        cost_estimate=cost(7.0),
        name="fill",
    )(spacing, anchor, reach, in_vmem(v), in_vmem(w), *sides, *ends, *late, *after)


def dot3(a_high, a_low, b_high, b_low, dims):
    def dot(a, b):
        return lax.dot_general(a, b, (dims, ((), ())), preferred_element_type=jnp.float32)

    return dot(a_high, b_high) + (dot(a_high, b_low) + dot(a_low, b_high))


def x_kernel(groups, made, step, c_high, c_low, *rest):
    pieces = rest[:groups]
    outs, (token, b_high, b_low, acc, sems) = rest[-5 - made : -5], rest[-5:]
    token[...] = jnp.zeros(token.shape, jnp.float32)
    apart = len(outs) > 1
    count, rows, _ = pieces[0].shape
    out_rows = outs[0].shape[-2]
    length = c_high.shape[0]
    parts = length // out_rows
    me = lax.axis_index("gx")
    for k in range(groups):
        at = pl.ds(pl.multiple_of((me ^ partner(k, groups)) * rows, rows), rows)
        for layer in range(count):
            high, low = split(pieces[k][layer])
            cols = pl.ds(layer * LANES, LANES)
            b_high[at, cols] = high
            b_low[at, cols] = low
    each = step // out_rows
    copies = []
    for tile in range(length // step):
        at = pl.ds(tile * step, step)
        value = dot3(c_high[at], c_low[at], b_high[...], b_low[...], ((1,), (0,)))
        if apart:
            acc[at] = value
            continue
        for part in range(each):
            for layer in range(count):
                acc[tile * each + part, layer] = value[
                    part * out_rows : (part + 1) * out_rows, layer * LANES : (layer + 1) * LANES
                ]
        some = pl.ds(tile * each, each)
        copies.append(pltpu.make_async_copy(acc.at[some], outs[0].at[some], sems.at[tile]))
        copies[-1].start()
    for copy in copies:
        copy.wait()
    if apart:
        row = lax.axis_index("gy")
        for k in range(parts):
            at = pl.ds(pl.multiple_of((row ^ partner(k, parts)) * out_rows, out_rows), out_rows)
            for layer in range(count):
                outs[k][layer] = acc[at, pl.ds(layer * LANES, LANES)]


def along_x(pieces, parts, apart, after):
    groups = len(pieces)
    count, rows, _ = pieces[0].shape
    length = rows * groups
    step = min(512 if apart else 256, length)
    high, low = cosine_split(length)
    tile = (count, length // parts, LANES)
    if apart:
        shapes = [jax.ShapeDtypeStruct(tile, jnp.float32)] * parts
    else:
        shapes = [pltpu.HBM((parts,) + tile, jnp.float32)]
    return pl.pallas_call(
        functools.partial(x_kernel, groups, len(shapes), step),
        out_shape=shapes + [TOKEN],
        in_specs=[VMEM] * (2 + groups) + [ANY] * len(after),
        out_specs=[VMEM if apart else HBM] * len(shapes) + [VMEM],
        scratch_shapes=[
            pltpu.VMEM((length, count * LANES), jnp.bfloat16),
            pltpu.VMEM((length, count * LANES), jnp.bfloat16),
            pltpu.VMEM((length, count * LANES) if apart else (parts,) + tile, jnp.float32),
            pltpu.SemaphoreType.DMA((length // step,)),
        ],
        compiler_params=params(length),
        cost_estimate=cost(0.4 * count),
        name="along_x",
    )(high, low, *pieces, *after)


def column_tiles(length, step):
    return [part.T.reshape(length, -1, step).swapaxes(0, 1) for part in cosine_split(length)]


def y_part_kernel(parts, cosines, *rest):
    out, a_high, a_low = rest[-3:]
    steps = out.shape[0]
    early = early_pieces(parts)
    pieces = rest[:early]
    count, rows, _ = pieces[0].shape
    row = lax.axis_index("gy")
    for n in range(parts):
        cols = pl.ds(pl.multiple_of((row ^ partner(n, parts)) * LANES, LANES), LANES)
        for layer in range(count):
            at = pl.ds(layer * rows, rows)
            if n < early:
                a_high[at, cols], a_low[at, cols] = split(pieces[n][layer])
            else:
                a_high[at, cols] = jnp.zeros((rows, LANES), jnp.bfloat16)
                a_low[at, cols] = jnp.zeros((rows, LANES), jnp.bfloat16)
    for tile in range(steps):
        out[tile] = dot3(a_high[...], a_low[...], cosines[tile], cosines[steps + tile], ((1,), (0,)))


def along_y_part(tiles, pieces, parts, after):
    count, rows, _ = pieces[0].shape
    _, length, step = tiles.shape
    return pl.pallas_call(
        functools.partial(y_part_kernel, parts),
        out_shape=jax.ShapeDtypeStruct((length // step, count * rows, step), jnp.float32),
        in_specs=[VMEM] * (1 + len(pieces)) + [ANY] * len(after),
        out_specs=VMEM,
        scratch_shapes=[pltpu.VMEM((count * rows, length), jnp.bfloat16)] * 2,
        compiler_params=params(length),
        cost_estimate=cost(2.0),
        name="along_y_part",
    )(in_vmem(tiles), *pieces, *after)


def y_rest_kernel(parts, slot, chained, spacing, anchor, cosines, partial, *rest):
    out, acc, table, sems = rest[-4:]
    early = early_pieces(parts)
    pieces = rest[: parts - early]
    steps = partial.shape[0]
    step = partial.shape[2]
    count, rows, _ = pieces[0].shape
    depth = out.shape[0]
    first = lax.axis_index("gx") * depth
    order_layers(table, 0, first, depth, spacing[0], anchor[0])
    row = lax.axis_index("gy")
    halves, places = [], []
    for n, piece in enumerate(pieces):
        halves.append(split(jnp.concatenate([piece[layer] for layer in range(count)], axis=0)))
        start = (row ^ partner(early + n, parts)) * LANES
        places.append(pl.ds(pl.multiple_of(start, LANES), LANES))
    copies = []
    for tile in range(steps):
        value = partial[tile]
        for (high, low), at in zip(halves, places):
            value = value + dot3(high, low, cosines[tile, at], cosines[steps + tile, at], ((1,), (0,)))
        acc[tile] = value
        for layer in range(count):
            copies.append(
                pltpu.make_async_copy(
                    acc.at[tile, pl.ds(layer * rows, rows)],
                    out.at[table[slot + layer] - first, :, pl.ds(tile * step, step)],
                    sems.at[tile, layer],
                )
            )
            copies[-1].start()
    for copy in copies:
        copy.wait()


def along_y_rest(tiles, spacing, anchor, partial, pieces, slot, depth, before, parts):
    count, rows, _ = pieces[0].shape
    _, length, step = tiles.shape
    steps = length // step
    chained = before is not None
    return pl.pallas_call(
        functools.partial(y_rest_kernel, parts, slot, chained),
        out_shape=jax.ShapeDtypeStruct((depth, rows, length), jnp.float32),
        in_specs=[SMEM, SMEM] + [VMEM] * (2 + len(pieces)) + ([HBM] if chained else []),
        out_specs=HBM,
        scratch_shapes=[
            pltpu.VMEM((steps, count * rows, step), jnp.float32),
            pltpu.SMEM((depth,), jnp.int32),
            pltpu.SemaphoreType.DMA((steps, count)),
        ],
        input_output_aliases={4 + len(pieces): 0} if chained else {},
        compiler_params=params(length),
        cost_estimate=cost(2.0),
        name="along_y_rest",
    )(spacing, anchor, in_vmem(tiles), partial, *pieces, *([before] if chained else []))


def y_kernel(slot, chained, apart, spacing, anchor, cosines, *rest):
    out, token, a_high, a_low, acc, near, table, sems, more = rest[-9:]
    _, length, step = cosines.shape
    steps = length // step
    parts = length // LANES
    pieces = rest[: parts if apart else 1]
    token[...] = jnp.zeros(token.shape, jnp.float32)
    count, rows, _ = pieces[0].shape[-3:]
    depth = out.shape[0]
    if not apart:
        arrivals = [pltpu.make_async_copy(pieces[0].at[n], near.at[n], more.at[n]) for n in range(parts)]
        for arrival in arrivals:
            arrival.start()
    first = lax.axis_index("gx") * depth
    order_layers(table, 0, first, depth, spacing[0], anchor[0])
    row = lax.axis_index("gy")
    for part in range(parts):
        if apart:
            piece = pieces[part]
            cols = pl.ds(pl.multiple_of((row ^ partner(part, parts)) * LANES, LANES), LANES)
        else:
            arrivals[part].wait()
            piece = near.at[part]
            cols = pl.ds(part * LANES, LANES)
        for layer in range(count):
            high, low = split(piece[layer])
            at = pl.ds(layer * rows, rows)
            a_high[at, cols] = high
            a_low[at, cols] = low

    copies = []
    for tile in range(steps):
        acc[tile] = dot3(a_high[...], a_low[...], cosines[tile], cosines[steps + tile], ((1,), (0,)))
        for layer in range(count):
            copies.append(
                pltpu.make_async_copy(
                    acc.at[tile, pl.ds(layer * rows, rows)],
                    out.at[table[slot + layer] - first, :, pl.ds(tile * step, step)],
                    sems.at[tile, layer],
                )
            )
            copies[-1].start()
    for copy in copies:
        copy.wait()


def along_y(tiles, spacing, anchor, pieces, slot, depth, before, parts, after):
    apart = len(pieces) > 1
    count, rows, _ = pieces[0].shape[-3:]
    length = parts * LANES
    step = min(256, length)
    steps = length // step
    chained = before is not None
    near = (1, 8, LANES) if apart else pieces[0].shape[1:]
    pieces = pieces if apart else [in_hbm(pieces[0])]
    return pl.pallas_call(
        functools.partial(y_kernel, slot, chained, apart),
        out_shape=[jax.ShapeDtypeStruct((depth, rows, length), jnp.float32), TOKEN],
        in_specs=[SMEM, SMEM, VMEM]
        + [VMEM if apart else HBM] * len(pieces)
        + ([HBM] if chained else [])
        + [ANY] * len(after),
        out_specs=[HBM, VMEM],
        scratch_shapes=[
            pltpu.VMEM((count * rows, length), jnp.bfloat16),
            pltpu.VMEM((count * rows, length), jnp.bfloat16),
            pltpu.VMEM((steps, count * rows, step), jnp.float32),
            pltpu.VMEM((1 if apart else parts,) + near, jnp.float32),
            pltpu.SMEM((depth,), jnp.int32),
            pltpu.SemaphoreType.DMA((steps, count)),
            pltpu.SemaphoreType.DMA((parts,)),
        ],
        input_output_aliases={3 + len(pieces): 0} if chained else {},
        compiler_params=params(length),
        cost_estimate=cost(1.0 * count),
        name="along_y",
    )(spacing, anchor, in_vmem(tiles), *pieces, *([before] if chained else []), *after)


def swap(value, axis, k):
    size = lax.axis_size(axis)
    return lax.ppermute(value, axis, [(i, i ^ k) for i in range(size)])


def exchange(pieces, axis):
    return [swap(piece, axis, k) for piece, k in zip(pieces, partners(len(pieces) + 1))]


def swap_neighbours(first, second, axis):
    size = lax.axis_size(axis)
    answers = []
    for value, start in ((first, 0), (second, 1)):
        pairs = [(i, i + 1) for i in range(start, size - 1, 2)]
        answers.append(lax.ppermute(value, axis, pairs + [(j, i) for i, j in pairs]))
    return answers


def per_device(intensity, weight, spacing, anchor, reach):
    layers, rows, _ = intensity.shape
    groups = lax.axis_size("gx")
    parts = lax.axis_size("gy")
    depth = layers // groups
    held = hole_slots(depth)
    full = (rows * groups, LANES * parts)

    clean = depth - held
    early = min(EARLY, clean)
    late = clean - early

    def to_rows(spectrum, apart):
        if apart:
            return spectrum[:1] + exchange(spectrum[1:], "gy")
        return [lax.all_to_all(spectrum[0], "gy", split_axis=0, concat_axis=0, tiled=True)]

    chunks = []
    if early:
        gathered = gather_clean(spacing, anchor, intensity, groups, 0, early)
        first_pieces = exchange(gathered, "gx")
    v, w, own, one, other, *mine, token = punch(
        spacing, anchor, reach, intensity, weight, groups, held, early, late
    )
    sides = swap_neighbours(one, other, "gy")
    ends = swap_neighbours(*edges(v, w, own, *sides, []), "gx")
    if early:
        first_pieces = mine[:1] + first_pieces
        mine = mine[1:]
        *spectrum, token = along_x(first_pieces, parts, FIRST_APART, sides)
        chunks.append((0, to_rows(spectrum, FIRST_APART)))
    *filled, token = fill(
        spacing, anchor, reach, v, w, [own] + sides, ends, mine, groups, held, depth, full, [token]
    )
    tiles = jnp.asarray(np.concatenate(column_tiles(full[1], min(256, full[1]))))
    pieces = filled[:1] + exchange([filled[k] for k in partners(groups)], "gx")
    *spectrum, token = along_x(pieces, parts, LAST_APART, [token])
    chunks.append((early, to_rows(spectrum, LAST_APART)))
    out = None
    for slot, pieces in chunks[:-1]:
        out, token = along_y(tiles, spacing, anchor, pieces, slot, depth, out, parts, [token])
    slot, pieces = chunks[-1]
    some = early_pieces(parts)
    partial = along_y_part(tiles, pieces[:some], parts, [token])
    out = along_y_rest(tiles, spacing, anchor, partial, pieces[some:], slot, depth, out, parts)
    return out


def solution(mesh):
    in_specs = (P(None, "gx", "gy"), P(None, "gx", "gy"), P(), P(), P())
    out_specs = P("gx", "gy", None)
    return jax.shard_map(per_device, mesh=mesh, in_specs=in_specs, out_specs=out_specs, check_vma=False)
```
